256 devices in a mesh: dp: 4 (over y), pipe: 4 (over x_hi, core), tensor: 16 (over z, x_lo).
Axes of the slice: x: 4 (x_hi: 2, x_lo: 2; x = x_hi * 2 + x_lo), y: 4, z: 8, core: 2. Of those that a mesh axis runs over, the one named last changes fastest.
Arguments:
- inputs: bfloat16 [2, 512, 8192], P(None, 'dp', 'tensor'), may hold values from -6 to 6
- cotangent: bfloat16 [2, 512, 8192], P(None, 'dp', 'tensor'), may hold values from -0.19921875 to 0.19921875
- up_weight: bfloat16 [4, 32, 6, 256, 256], P('pipe', 'tensor'), may hold values from -0.15625 to 0.15625
- down_weight: bfloat16 [4, 32, 6, 256, 256], P('pipe', 'tensor'), may hold values from -0.15625 to 0.15625
Outputs:
- up_grad: float32 [4, 32, 6, 256, 256], P('pipe', 'tensor')
- down_grad: float32 [4, 32, 6, 256, 256], P('pipe', 'tensor')
The draws below stay inside these ranges and needn't reach their ends.
All inputs are finite; a program needn't handle non-finite values.
Results may differ from the reference program's by a relative error of at most 0.02.
Values may be sent and summed in bfloat16 or wider, within the bound.
No kernel may reach another device: no remote copies, remote signals or barrier semaphores. Data moves between devices by JAX's collectives and lax.ppermute only.
A program may use at most 64 MiB of HBM per device.

```python
import jax
import jax.numpy as jnp
from jax import lax

D = 8192
BS = 256
NB = 32
OFFS = 6
MICRO = 2
TOK = 512
LAYERS = 4


def steps_of(rng, dims, split, smallest, largest):
    gain, own = 1.0, jax.random.fold_in(rng, 6)
    for dim, shards_of in split:
        steps = jnp.exp(jax.random.uniform(jax.random.fold_in(own, dim), (shards_of,), jnp.float32, smallest / len(split), largest / len(split)))
        gain = gain * jnp.repeat(steps, dims[dim] // shards_of).reshape([-1 if axis == dim else 1 for axis in range(len(dims))])
    return gain


def noise(key, shape, deviation, bound, split=(), held_as=jnp.bfloat16):
    entries = deviation * jax.random.normal(key, shape, jnp.float32)
    if split:
        entries = entries * steps_of(key, shape, split, -0.22, 0.18)
    return jnp.clip(entries, -bound, bound).astype(held_as)


def setup_inputs(seed: int = 0) -> dict:
    key_of = jax.random.split(jax.random.key(seed), 5)
    return {
        "inputs": noise(key_of[0], (MICRO, TOK, D), 1.0, 6.0, ((1, 4), (2, 16))),
        "cotangent": noise(key_of[1], (MICRO, TOK, D), 0.03, 0.19921875, ((1, 4), (2, 16))),
        "up_weight": noise(key_of[2], (LAYERS, NB, OFFS, BS, BS), (OFFS * BS) ** -0.5, 0.15625, ((0, 4), (1, 16))),
        "down_weight": noise(key_of[3], (LAYERS, NB, OFFS, BS, BS), (OFFS * BS) ** -0.5, 0.15625, ((0, 4), (1, 16))),
    }


ROOT_HALF = 0.7071067811865476
INV_ROOT_TWO_PI = 0.3989422804014327


def offsets_table(count):
    return [0] + [2 ** j for j in range(count - 1)]


def gelu_value(v):
    return v * 0.5 * (1.0 + lax.erf(v * ROOT_HALF))


def gelu_slope(v):
    return 0.5 * (1.0 + lax.erf(v * ROOT_HALF)) + v * INV_ROOT_TWO_PI * jnp.exp(-0.5 * v * v)


def partner_index(blocks, count):
    rows_idx = jnp.arange(blocks, dtype=jnp.int32)[:, None]
    shifts = jnp.array(offsets_table(count), dtype=jnp.int32)[None, :]
    return jnp.bitwise_xor(rows_idx, shifts).astype(jnp.int32)


def butterfly(weight, values, index):
    gathered = values[:, index].astype(jnp.float32)
    return jnp.einsum("tnkb,nkbc->tnc", gathered, weight.astype(jnp.float32), precision=lax.Precision.HIGHEST)


def butterfly_t(weight, grads, index, columns):
    gathered = grads[:, index].astype(jnp.float32)
    moved = weight[index, columns].astype(jnp.float32)
    return jnp.einsum("tnkc,nkbc->tnb", gathered, moved, precision=lax.Precision.HIGHEST)


def outer_blocks(values, grads, index):
    gathered = values[:, index].astype(jnp.float32)
    return jnp.einsum("tnkb,tnc->nkbc", gathered, grads.astype(jnp.float32), precision=lax.Precision.HIGHEST)


def reference(inputs, cotangent, up_weight, down_weight):
    index = partner_index(NB, OFFS)
    columns = jnp.arange(OFFS, dtype=jnp.int32)[None, :]
    up_grad = jnp.zeros((LAYERS, NB, OFFS, BS, BS), jnp.float32)
    down_grad = jnp.zeros((LAYERS, NB, OFFS, BS, BS), jnp.float32)
    for micro_idx in range(MICRO):
        layer_in = inputs[micro_idx].reshape(TOK, NB, BS)
        saved_in, saved_hidden, saved_act = [], [], []
        for layer in range(LAYERS):
            hidden = butterfly(up_weight[layer], layer_in, index)
            act = gelu_value(hidden).astype(jnp.bfloat16)
            saved_in.append(layer_in)
            saved_hidden.append(hidden)
            saved_act.append(act)
            layer_in = (layer_in.astype(jnp.float32) + butterfly(down_weight[layer], act, index)).astype(jnp.bfloat16)
        grads = cotangent[micro_idx].reshape(TOK, NB, BS)
        for layer in range(LAYERS - 1, -1, -1):
            grad_act = butterfly_t(down_weight[layer], grads, index, columns)
            grad_hidden = (grad_act * gelu_slope(saved_hidden[layer])).astype(jnp.bfloat16)
            down_grad = down_grad.at[layer].add(outer_blocks(saved_act[layer], grads, index))
            up_grad = up_grad.at[layer].add(outer_blocks(saved_in[layer], grad_hidden, index))
            grads = (grads.astype(jnp.float32) + butterfly_t(up_weight[layer], grad_hidden, index, columns)).astype(jnp.bfloat16)
    return up_grad, down_grad
```

```python
import functools

import jax
import jax.numpy as jnp
from jax import lax
from jax.experimental import pallas as pl
from jax.experimental.pallas import tpu as pltpu
from jax.sharding import PartitionSpec as P

ROOT_HALF = 0.7071067811865476
INV_ROOT_TWO_PI = 0.3989422804014327
BS = 256
BF = jnp.bfloat16
F32 = jnp.float32
ANY = pl.BlockSpec(memory_space=pl.ANY)
VMEM = pl.BlockSpec(memory_space=pltpu.VMEM)
HBM = pl.BlockSpec(memory_space=pltpu.HBM)
NN = (((1,), (0,)), ((), ()))
NT = (((1,), (1,)), ((), ()))
TN = (((0,), (0,)), ((), ()))


def dot(a, b, dims):
    return lax.dot_general(a, b, dims, preferred_element_type=F32)


def flip(x, axis, bit):
    n = lax.axis_size(axis)
    return lax.ppermute(x, axis, [(i, i ^ bit) for i in range(n)])


def after(x, *events):
    return lax.optimization_barrier((x,) + events)[0]


def partners(arrays):
    return [flip(a, "tensor", 1 << b) for b, a in enumerate(arrays)]


def fetch(which, sources, wbuf, sems):
    for s, src in enumerate(sources):

        @pl.when(which == s)
        def _():
            for j in range(2):
                pltpu.make_async_copy(src.at[j], wbuf.at[j], sems.at[j]).start()


def arrived(j, sources, wbuf, sems):
    pltpu.make_async_copy(sources[0].at[j], wbuf.at[j], sems.at[j]).wait()
    return wbuf[j].reshape(6 * BS, BS)


def own_and_partner(j, own, recv):
    cols = pl.ds(j * BS, BS)
    flipped = pl.ds((1 - j) * BS, BS)
    return jnp.concatenate([own[:, cols], own[:, flipped]] + [r[:, cols] for r in recv], axis=1)


def stack_copies(own, recv, stack, sem):
    return [pltpu.make_async_copy(src, stack.at[i], sem.at[i]) for i, src in enumerate([own] + recv)]


def layer_source(q, keep):
    p = lax.axis_index("pipe")
    return (p % 2) ^ q, p // 2 if keep else 1


def up_kernel(n_src, keep, q, *refs):
    which, write = layer_source(q, keep)
    own, recv, refs = refs[0], list(refs[1:5]), refs[5:]
    sources, refs = refs[:n_src], refs[n_src:]
    if keep:
        (_, old_slope), refs = refs[:2], refs[2:]
    act, slope, stack, wbuf, sems, ssem = refs
    fetch(which, sources, wbuf, sems)
    copies = stack_copies(own, recv, stack, ssem)

    @pl.when(write == 1)
    def _():
        for cp in copies:
            cp.start()

    for j in range(2):
        x = own_and_partner(j, own, recv)
        w = arrived(j, sources, wbuf, sems)
        hid = dot(x, w, NN)
        cdf = 0.5 * (1.0 + lax.erf(hid * ROOT_HALF))
        cols = pl.ds(j * BS, BS)
        act[:, cols] = (hid * cdf).astype(BF)
        s = (cdf + hid * INV_ROOT_TWO_PI * jnp.exp(-0.5 * hid * hid)).astype(BF)
        if keep:
            s = jnp.where(write == 1, s, old_slope[:, cols])
        slope[:, cols] = s

    @pl.when(write == 1)
    def _():
        for cp in copies:
            cp.wait()


def down_kernel(n_src, keep, q, *refs):
    which, write = layer_source(q, keep)
    z, own, recv, refs = refs[0], refs[1], list(refs[2:6]), refs[6:]
    sources, refs = refs[:n_src], refs[n_src:]
    if keep:
        refs = refs[1:]
    znew, stack, wbuf, sems, ssem = refs
    fetch(which, sources, wbuf, sems)
    copies = stack_copies(own, recv, stack, ssem)

    @pl.when(write == 1)
    def _():
        for cp in copies:
            cp.start()

    for j in range(2):
        x = own_and_partner(j, own, recv)
        w = arrived(j, sources, wbuf, sems)
        cols = pl.ds(j * BS, BS)
        znew[:, cols] = (z[:, cols].astype(F32) + dot(x, w, NN)).astype(BF)

    @pl.when(write == 1)
    def _():
        for cp in copies:
            cp.wait()


def stack_kernel(own, r0, r1, r2, r3, _, stack, ssem):
    write = lax.axis_index("pipe") // 2
    copies = stack_copies(own, [r0, r1, r2, r3], stack, ssem)

    @pl.when(write == 1)
    def _():
        for cp in copies:
            cp.start()
        for cp in copies:
            cp.wait()


def products(g, sources, wbuf, sems, part, outs):
    rows = g.shape[0]
    acc = [None, None]
    for j in range(2):
        w = arrived(j, sources, wbuf, sems)
        t = dot(g[:, j * BS : (j + 1) * BS], w, NT)
        acc[j] = t[:, :BS] if acc[j] is None else acc[j] + t[:, :BS]
        other = t[:, BS : 2 * BS]
        acc[1 - j] = other if acc[1 - j] is None else acc[1 - j] + other
        for k, o in enumerate(outs):
            o[:, j * BS : (j + 1) * BS] = t[:, (k + 2) * BS : (k + 3) * BS].astype(BF)
    for j in range(2):
        part[:, j * BS : (j + 1) * BS] = acc[j]


def first_kernel(layer, g, s0, s1, s2, s3, part, o0, o1, o2, o3, wbuf, sems):
    sources = (s0, s1, s2, s3)
    fetch(lax.axis_index("pipe") ^ layer, sources, wbuf, sems)
    products(g[...], sources, wbuf, sems, part, (o0, o1, o2, o3))


def total(part, recv):
    s = part[...]
    for r in recv:
        s = s + r[...].astype(F32)
    return s


def mid_kernel(layer, part, r0, r1, r2, r3, slope, s0, s1, s2, s3, gh, newpart, o0, o1, o2, o3, wbuf, sems):
    sources = (s0, s1, s2, s3)
    fetch(lax.axis_index("pipe") ^ layer, sources, wbuf, sems)
    v = (total(part, (r0, r1, r2, r3)) * slope[...].astype(F32)).astype(BF)
    gh[...] = v
    products(v, sources, wbuf, sems, newpart, (o0, o1, o2, o3))


def end_kernel(layer, part, r0, r1, r2, r3, g, s0, s1, s2, s3, gnew, newpart, o0, o1, o2, o3, wbuf, sems):
    sources = (s0, s1, s2, s3)
    fetch(lax.axis_index("pipe") ^ layer, sources, wbuf, sems)
    v = (total(part, (r0, r1, r2, r3)) + g[...].astype(F32)).astype(BF)
    gnew[...] = v
    products(v, sources, wbuf, sems, newpart, (o0, o1, o2, o3))


def last_kernel(part, r0, r1, r2, r3, slope, gh):
    gh[...] = (total(part, (r0, r1, r2, r3)) * slope[...].astype(F32)).astype(BF)


def grad_kernel(g_own, g_oth, *refs):
    choices, (out, buf, sems) = refs[:8], refs[8:]
    for which in range(2):

        @pl.when(lax.axis_index("pipe") % 2 == which)
        def _():
            for i in range(4):
                pltpu.make_async_copy(choices[2 * i + which], buf.at[i], sems.at[i]).start()

    for ud in range(2):
        for i in (2 * ud, 2 * ud + 1):
            pltpu.make_async_copy(choices[2 * i], buf.at[i], sems.at[i]).wait()
        first = 512 if ud == 0 else 0
        for j in range(2):
            cols = pl.ds(j * BS, BS)
            for k in range(6):
                src = 0 if k < 2 else k - 1
                xc = pl.ds((1 - j if k == 1 else j) * BS, BS)
                acc = dot(buf[2 * ud, src, :, xc], g_own[:, first + j * BS : first + (j + 1) * BS], TN)
                acc = acc + dot(buf[2 * ud + 1, src, :, xc], g_oth[:, first + j * BS : first + (j + 1) * BS], TN)
                out[2 * j + k // 3, ud, (k % 3) * BS : (k % 3 + 1) * BS, :] = acc.astype(BF)


def place_kernel(q0, q1, q2, q3, up, down):
    for k, q in enumerate((q0, q1, q2, q3)):
        rows = pl.ds(pl.multiple_of((lax.axis_index("dp") ^ k) * 3 * BS, 3 * BS), 3 * BS)
        up[rows, :] = q[0].astype(F32)
        down[rows, :] = q[1].astype(F32)


def call(body, outs, ins, scratch=(), any_in=(), hbm_in=(), hbm_out=(), aliases=None, flops=0, nbytes=0, limit=12 << 20):
    return pl.pallas_call(
        body,
        out_shape=[jax.ShapeDtypeStruct(s, t) for s, t in outs],
        in_specs=[ANY if i in any_in else HBM if i in hbm_in else VMEM for i in range(len(ins))],
        out_specs=[HBM if i in hbm_out else VMEM for i in range(len(outs))],
        scratch_shapes=list(scratch),
        input_output_aliases=aliases or {},
        compiler_params=pltpu.CompilerParams(vmem_limit_bytes=limit),
        cost_estimate=pl.CostEstimate(flops=flops, bytes_accessed=nbytes, transcendentals=0),
    )(*ins)


W_SCRATCH = [pltpu.VMEM((2, 6, BS, BS), BF), pltpu.SemaphoreType.DMA((2,))]
S_SCRATCH = [pltpu.SemaphoreType.DMA((5,))]
W_BYTES = 12 * BS * BS * 2


def per_device(inputs, cotangent, up_weight, down_weight):
    p = lax.axis_index("pipe")
    d = lax.axis_index("dp")
    h, c = p // 2, p % 2
    rows, width = inputs.shape[1], inputs.shape[2]
    half = rows // 2
    shape, half_shape = (rows, width), (half, width)
    flops = 2 * rows * 6 * BS * width

    ups, downs = [up_weight[0]], [down_weight[0]]

    def fwd_up(stage, q, z, recv):
        keep = stage == 1
        return call(
            functools.partial(up_kernel, 2, keep, q),
            [(shape, BF), (shape, BF), ((5,) + shape, BF)],
            [z] + recv + ups[:2] + ([zst[q], slopes[q]] if keep else []),
            W_SCRATCH + S_SCRATCH,
            hbm_in=(5, 6, 7),
            hbm_out=(2,),
            aliases={7: 2} if keep else None,
            flops=flops,
            nbytes=2 * W_BYTES,
        )

    def fwd_down(stage, q, z, act, recv):
        keep = stage == 1
        return call(
            functools.partial(down_kernel, 2, keep, q),
            [(shape, BF), ((5,) + shape, BF)],
            [z, act] + recv + downs[:2] + ([ast[q]] if keep else []),
            W_SCRATCH + S_SCRATCH,
            hbm_in=(6, 7, 8),
            hbm_out=(1,),
            aliases={8: 1} if keep else None,
            flops=flops,
            nbytes=2 * W_BYTES,
        )

    slopes, zst, ast = [None, None], [None, None], [None, None]
    z = lax.dynamic_index_in_dim(inputs, c, 0, keepdims=False)
    recv = partners([z] * 4)
    ups.append(flip(after(ups[0], z), "pipe", 1))
    act, slopes[0], zst[0] = fwd_up(0, 0, z, recv)
    recv = partners([act] * 4)
    downs.append(flip(after(downs[0], act), "pipe", 1))
    z, ast[0] = fwd_down(0, 0, z, act, recv)
    recv = partners([z] * 4)
    downs.append(flip(after(downs[0], z), "pipe", 2))
    act, slopes[1], zst[1] = fwd_up(0, 1, z, recv)
    recv = partners([act] * 4)
    z, ast[1] = fwd_down(0, 1, z, act, recv)
    downs.append(flip(after(downs[2], act), "pipe", 1))
    g = lax.dynamic_slice_in_dim(lax.dynamic_index_in_dim(cotangent, c, 0, keepdims=False), h * half, half, 0)
    part_outs = [(half_shape, F32)] + [(half_shape, BF)] * 4
    part, *outs = call(
        functools.partial(first_kernel, 3), part_outs, [after(g, z)] + downs, W_SCRATCH,
        hbm_in=(1, 2, 3, 4), flops=flops // 2, nbytes=W_BYTES,
    )
    z = flip(z, "pipe", 2)
    first_recv = partners(outs)
    recv = partners([z] * 4)
    ups.append(flip(after(ups[0], z), "pipe", 2))
    act, slopes[0], zst[0] = fwd_up(1, 0, z, recv)
    recv = partners([act] * 4)
    z, ast[0] = fwd_down(1, 0, z, act, recv)
    recv = partners([z] * 4)
    ups.append(flip(after(ups[2], z), "pipe", 1))
    act, slopes[1], zst[1] = fwd_up(1, 1, z, recv)

    both = jnp.stack(slopes)
    mine = lax.dynamic_slice_in_dim(both, h * half, half, 1)
    got = flip(lax.dynamic_slice_in_dim(both, (1 - h) * half, half, 1), "pipe", 2)
    low, high = jnp.where(h == 0, mine, got), jnp.where(h == 0, got, mine)
    slope = [low[0], low[1], high[0], high[1]]

    pairs = [None] * 4
    act_recv = []
    zsw, asw = [None] * 2, [None] * 2
    for layer in (3, 2, 1, 0):
        recv = first_recv if layer == 3 else partners(outs)
        if layer == 0:
            zsw[1] = flip(after(zst[1], part), "pipe", 1)
            (ast[1],) = call(
                stack_kernel, [((5,) + shape, BF)], [act] + act_recv + [ast[1]], S_SCRATCH,
                hbm_in=(5,), hbm_out=(0,), aliases={5: 0}, nbytes=W_BYTES,
            )
            asw[1] = flip(after(ast[1], part), "pipe", 1)
            (gh,) = call(last_kernel, [(half_shape, BF)], [part] + recv + [slope[0]], nbytes=1 << 18)
            pairs[0] = (g, gh)
            break
        gh, part, *outs = call(
            functools.partial(mid_kernel, layer), [(half_shape, BF)] + part_outs,
            [part] + recv + [slope[layer]] + ups, W_SCRATCH,
            hbm_in=(6, 7, 8, 9), flops=flops // 2, nbytes=W_BYTES,
        )
        pairs[layer] = (g, gh)
        recv = partners(outs)
        if layer > 1:
            act_recv.append(flip(after(act, part), "tensor", 1 << len(act_recv)))
        else:
            zsw[0] = flip(after(zst[0], part), "pipe", 1)
            asw[0] = flip(after(ast[0], part, zsw[0]), "pipe", 1)
        g, part, *outs = call(
            functools.partial(end_kernel, layer - 1), [(half_shape, BF)] + part_outs,
            [part] + recv + [g] + downs, W_SCRATCH,
            hbm_in=(6, 7, 8, 9), flops=flops // 2, nbytes=W_BYTES,
        )
        if layer > 1:
            act_recv.append(flip(after(act, part), "tensor", 1 << len(act_recv)))

    packed = [jnp.concatenate(pr, axis=1) for pr in pairs]
    low, high = jnp.stack(packed[:2]), jnp.stack(packed[2:])
    mine = jnp.where(h == 0, low, high)
    got = flip(jnp.where(h == 0, high, low), "pipe", 2)
    full = jnp.where(h == 0, jnp.concatenate([mine, got], 1), jnp.concatenate([got, mine], 1))
    g_own = jnp.where(c == 0, full[0], full[1])
    g_oth = flip(jnp.where(c == 0, full[1], full[0]), "pipe", 1)
    (partial,) = call(
        grad_kernel,
        [((4, 2, 3 * BS, BS), BF)],
        [g_own, g_oth] + zst + zsw + ast + asw,
        [pltpu.VMEM((4, 5) + shape, BF), pltpu.SemaphoreType.DMA((4,))],
        hbm_in=tuple(range(2, 10)),
        flops=8 * flops,
        nbytes=6 << 20,
        limit=24 << 20,
    )
    acc = lax.dynamic_index_in_dim(partial, d, 0, keepdims=False).astype(F32)
    for k in (1, 2, 3):
        acc = acc + flip(lax.dynamic_index_in_dim(partial, d ^ k, 0, keepdims=False), "dp", k).astype(F32)
    acc = acc.astype(BF)
    quarters = [acc] + [flip(acc, "dp", k) for k in (1, 2, 3)]
    up, down = call(place_kernel, [((12 * BS, BS), F32)] * 2, quarters, nbytes=10 << 20, limit=24 << 20)
    out = (1, 2, 6, BS, BS)
    return up.reshape(out), down.reshape(out)


def solution(mesh):
    acts = P(None, "dp", "tensor")
    weights = P("pipe", "tensor", None, None, None)
    return jax.shard_map(
        per_device, mesh=mesh, in_specs=(acts, acts, weights, weights), out_specs=(weights, weights), check_vma=False
    )
```

```python
import functools

import jax
import jax.numpy as jnp
from jax import lax
from jax.experimental import pallas as pl
from jax.experimental.pallas import tpu as pltpu
from jax.sharding import PartitionSpec as P

ROOT_HALF = 0.7071067811865476
INV_ROOT_TWO_PI = 0.3989422804014327
BS = 256
BF = jnp.bfloat16
F32 = jnp.float32
ANY = pl.BlockSpec(memory_space=pl.ANY)
VMEM = pl.BlockSpec(memory_space=pltpu.VMEM)
HBM = pl.BlockSpec(memory_space=pltpu.HBM)
NN = (((1,), (0,)), ((), ()))
NT = (((1,), (1,)), ((), ()))
TN = (((0,), (0,)), ((), ()))


def dot(a, b, dims):
    return lax.dot_general(a, b, dims, preferred_element_type=F32)


def flip(x, axis, bit):
    n = lax.axis_size(axis)
    return lax.ppermute(x, axis, [(i, i ^ bit) for i in range(n)])


def after(x, *events):
    return lax.optimization_barrier((x,) + events)[0]


def partners(arrays):
    return [flip(a, "tensor", 1 << b) for b, a in enumerate(arrays)]


def fetch(which, sources, wbuf, sems):
    for s, src in enumerate(sources):

        @pl.when(which == s)
        def _():
            for j in range(2):
                pltpu.make_async_copy(src.at[j], wbuf.at[j], sems.at[j]).start()


def arrived(j, sources, wbuf, sems):
    pltpu.make_async_copy(sources[0].at[j], wbuf.at[j], sems.at[j]).wait()
    return wbuf[j].reshape(6 * BS, BS)


def own_and_partner(j, own, recv):
    cols = pl.ds(j * BS, BS)
    flipped = pl.ds((1 - j) * BS, BS)
    return jnp.concatenate([own[:, cols], own[:, flipped]] + [r[:, cols] for r in recv], axis=1)


def stack_copies(own, recv, stack, sem):
    return [pltpu.make_async_copy(src, stack.at[i], sem.at[i]) for i, src in enumerate([own] + recv)]


def layer_source(q, keep):
    p = lax.axis_index("pipe")
    return (p % 2) ^ q, p // 2 if keep else 1


def up_kernel(n_src, keep, q, *refs):
    which, write = layer_source(q, keep)
    own, recv, refs = refs[0], list(refs[1:5]), refs[5:]
    sources, refs = refs[:n_src], refs[n_src:]
    if keep:
        (_, old_slope), refs = refs[:2], refs[2:]
    act, slope, stack, wbuf, sems, ssem = refs
    fetch(which, sources, wbuf, sems)
    copies = stack_copies(own, recv, stack, ssem)

    @pl.when(write == 1)
    def _():
        for cp in copies:
            cp.start()

    for j in range(2):
        x = own_and_partner(j, own, recv)
        w = arrived(j, sources, wbuf, sems)
        hid = dot(x, w, NN)
        cdf = 0.5 * (1.0 + lax.erf(hid * ROOT_HALF))
        cols = pl.ds(j * BS, BS)
        act[:, cols] = (hid * cdf).astype(BF)
        s = (cdf + hid * INV_ROOT_TWO_PI * jnp.exp(-0.5 * hid * hid)).astype(BF)
        if keep:
            s = jnp.where(write == 1, s, old_slope[:, cols])
        slope[:, cols] = s

    @pl.when(write == 1)
    def _():
        for cp in copies:
            cp.wait()


def down_kernel(n_src, keep, q, *refs):
    which, write = layer_source(q, keep)
    z, own, recv, refs = refs[0], refs[1], list(refs[2:6]), refs[6:]
    sources, refs = refs[:n_src], refs[n_src:]
    if keep:
        refs = refs[1:]
    znew, stack, wbuf, sems, ssem = refs
    fetch(which, sources, wbuf, sems)
    copies = stack_copies(own, recv, stack, ssem)

    @pl.when(write == 1)
    def _():
        for cp in copies:
            cp.start()

    for j in range(2):
        x = own_and_partner(j, own, recv)
        w = arrived(j, sources, wbuf, sems)
        cols = pl.ds(j * BS, BS)
        znew[:, cols] = (z[:, cols].astype(F32) + dot(x, w, NN)).astype(BF)

    @pl.when(write == 1)
    def _():
        for cp in copies:
            cp.wait()


def stack_kernel(own, r0, r1, r2, r3, _, stack, ssem):
    write = lax.axis_index("pipe") // 2
    copies = stack_copies(own, [r0, r1, r2, r3], stack, ssem)

    @pl.when(write == 1)
    def _():
        for cp in copies:
            cp.start()
        for cp in copies:
            cp.wait()


def fetch_layer(layer, wall, wbuf, sems):
    for j in range(2):
        pltpu.make_async_copy(wall.at[layer, j], wbuf.at[j], sems.at[j]).start()


def products(g, wall, wbuf, sems, part, outs):
    rows = g.shape[0]
    acc = [None, None]
    for j in range(2):
        w = arrived(j, [wall.at[0]], wbuf, sems)
        t = dot(g[:, j * BS : (j + 1) * BS], w, NT)
        acc[j] = t[:, :BS] if acc[j] is None else acc[j] + t[:, :BS]
        other = t[:, BS : 2 * BS]
        acc[1 - j] = other if acc[1 - j] is None else acc[1 - j] + other
        for k, o in enumerate(outs):
            o[:, j * BS : (j + 1) * BS] = t[:, (k + 2) * BS : (k + 3) * BS].astype(BF)
    for j in range(2):
        part[:, j * BS : (j + 1) * BS] = acc[j]


def first_kernel(layer, g, wall, part, o0, o1, o2, o3, wbuf, sems):
    fetch_layer(layer, wall, wbuf, sems)
    products(g[...], wall, wbuf, sems, part, (o0, o1, o2, o3))


def total(part, recv):
    s = part[...]
    for r in recv:
        s = s + r[...].astype(F32)
    return s


def mid_kernel(layer, part, r0, r1, r2, r3, slope, wall, gh, newpart, o0, o1, o2, o3, wbuf, sems):
    fetch_layer(layer, wall, wbuf, sems)
    v = (total(part, (r0, r1, r2, r3)) * slope[...].astype(F32)).astype(BF)
    gh[...] = v
    products(v, wall, wbuf, sems, newpart, (o0, o1, o2, o3))


def end_kernel(layer, part, r0, r1, r2, r3, g, wall, gnew, newpart, o0, o1, o2, o3, wbuf, sems):
    fetch_layer(layer, wall, wbuf, sems)
    v = (total(part, (r0, r1, r2, r3)) + g[...].astype(F32)).astype(BF)
    gnew[...] = v
    products(v, wall, wbuf, sems, newpart, (o0, o1, o2, o3))


def last_kernel(part, r0, r1, r2, r3, slope, gh):
    gh[...] = (total(part, (r0, r1, r2, r3)) * slope[...].astype(F32)).astype(BF)


def grad_kernel(g_own, g_oth, *refs):
    choices, (out, buf, sems) = refs[:8], refs[8:]
    for which in range(2):

        @pl.when(lax.axis_index("pipe") % 2 == which)
        def _():
            for i in range(4):
                pltpu.make_async_copy(choices[2 * i + which], buf.at[i], sems.at[i]).start()

    for ud in range(2):
        for i in (2 * ud, 2 * ud + 1):
            pltpu.make_async_copy(choices[2 * i], buf.at[i], sems.at[i]).wait()
        first = 512 if ud == 0 else 0
        for j in range(2):
            cols = pl.ds(j * BS, BS)
            for k in range(6):
                src = 0 if k < 2 else k - 1
                xc = pl.ds((1 - j if k == 1 else j) * BS, BS)
                acc = dot(buf[2 * ud, src, :, xc], g_own[:, first + j * BS : first + (j + 1) * BS], TN)
                acc = acc + dot(buf[2 * ud + 1, src, :, xc], g_oth[:, first + j * BS : first + (j + 1) * BS], TN)
                out[2 * j + k // 3, ud, (k % 3) * BS : (k % 3 + 1) * BS, :] = acc.astype(BF)


def place_kernel(q0, q1, q2, q3, up, down):
    for k, q in enumerate((q0, q1, q2, q3)):
        rows = pl.ds(pl.multiple_of((lax.axis_index("dp") ^ k) * 3 * BS, 3 * BS), 3 * BS)
        up[rows, :] = q[0].astype(F32)
        down[rows, :] = q[1].astype(F32)


def call(body, outs, ins, scratch=(), any_in=(), hbm_in=(), hbm_out=(), aliases=None, flops=0, nbytes=0, limit=12 << 20):
    return pl.pallas_call(
        body,
        out_shape=[pltpu.HBM(s, t) if i in hbm_out else jax.ShapeDtypeStruct(s, t) for i, (s, t) in enumerate(outs)],
        in_specs=[ANY if i in any_in else HBM if i in hbm_in else VMEM for i in range(len(ins))],
        out_specs=[HBM if i in hbm_out else VMEM for i in range(len(outs))],
        scratch_shapes=list(scratch),
        input_output_aliases=aliases or {},
        compiler_params=pltpu.CompilerParams(vmem_limit_bytes=limit),
        cost_estimate=pl.CostEstimate(flops=flops, bytes_accessed=nbytes, transcendentals=0),
    )(*[pltpu.with_memory_space_constraint(x, pltpu.HBM) if i in hbm_in else x for i, x in enumerate(ins)])


W_SCRATCH = [pltpu.VMEM((2, 6, BS, BS), BF), pltpu.SemaphoreType.DMA((2,))]
S_SCRATCH = [pltpu.SemaphoreType.DMA((5,))]
W_BYTES = 12 * BS * BS * 2


def per_device(inputs, cotangent, up_weight, down_weight):
    p = lax.axis_index("pipe")
    d = lax.axis_index("dp")
    h, c = p // 2, p % 2
    rows, width = inputs.shape[1], inputs.shape[2]
    half = rows // 2
    shape, half_shape = (rows, width), (half, width)
    flops = 2 * rows * 6 * BS * width

    ups, downs = [up_weight[0]], [down_weight[0]]
    all_down = lax.all_gather(downs[0], "pipe")

    def fwd_up(stage, q, z, recv):
        keep = stage == 1
        return call(
            functools.partial(up_kernel, 2, keep, q),
            [(shape, BF), (shape, BF), ((5,) + shape, BF)],
            [z] + recv + ups[:2] + ([zst[q], slopes[q]] if keep else []),
            W_SCRATCH + S_SCRATCH,
            hbm_in=(5, 6, 7),
            hbm_out=(2,),
            aliases={7: 2} if keep else None,
            flops=flops,
            nbytes=2 * W_BYTES,
        )

    def fwd_down(stage, q, z, act, recv):
        keep = stage == 1
        return call(
            functools.partial(down_kernel, 2, keep, q),
            [(shape, BF), ((5,) + shape, BF)],
            [z, act] + recv + downs[:2] + ([ast[q]] if keep else []),
            W_SCRATCH + S_SCRATCH,
            hbm_in=(6, 7, 8),
            hbm_out=(1,),
            aliases={8: 1} if keep else None,
            flops=flops,
            nbytes=2 * W_BYTES,
        )

    slopes, zst, ast = [None, None], [None, None], [None, None]
    z = lax.dynamic_index_in_dim(inputs, c, 0, keepdims=False)
    recv = partners([z] * 4)
    ups.append(flip(after(ups[0], z), "pipe", 1))
    act, slopes[0], zst[0] = fwd_up(0, 0, z, recv)
    recv = partners([act] * 4)
    downs.append(flip(after(downs[0], act), "pipe", 1))
    z, ast[0] = fwd_down(0, 0, z, act, recv)
    recv = partners([z] * 4)
    act, slopes[1], zst[1] = fwd_up(0, 1, z, recv)
    recv = partners([act] * 4)
    z, ast[1] = fwd_down(0, 1, z, act, recv)
    g = lax.dynamic_slice_in_dim(lax.dynamic_index_in_dim(cotangent, c, 0, keepdims=False), h * half, half, 0)
    part_outs = [(half_shape, F32)] + [(half_shape, BF)] * 4
    part, *outs = call(
        functools.partial(first_kernel, 3), part_outs, [after(g, act), all_down], W_SCRATCH,
        hbm_in=(1,), flops=flops // 2, nbytes=W_BYTES,
    )
    z = after(flip(z, "pipe", 2), part)
    first_recv = partners(outs)
    z = after(z, *first_recv)
    all_up = lax.all_gather(after(ups[0], z), "pipe")
    recv = partners([z] * 4)
    act, slopes[0], zst[0] = fwd_up(1, 0, z, recv)
    recv = partners([act] * 4)
    z, ast[0] = fwd_down(1, 0, z, act, recv)
    recv = partners([z] * 4)
    act, slopes[1], zst[1] = fwd_up(1, 1, z, recv)

    both = jnp.stack(slopes)
    mine = lax.dynamic_slice_in_dim(both, h * half, half, 1)
    got = flip(lax.dynamic_slice_in_dim(both, (1 - h) * half, half, 1), "pipe", 2)
    low, high = jnp.where(h == 0, mine, got), jnp.where(h == 0, got, mine)
    slope = [low[0], low[1], high[0], high[1]]

    pairs = [None] * 4
    act_recv = []
    zsw, asw = [None] * 2, [None] * 2
    for layer in (3, 2, 1, 0):
        recv = first_recv if layer == 3 else partners(outs)
        if layer in (1, 2):
            act_recv.append(flip(after(act, part), "tensor", 1 << len(act_recv)))
            part = after(part, act_recv[-1])
        if layer == 0:
            zsw[1] = flip(after(zst[1], part), "pipe", 1)
            (ast[1],) = call(
                stack_kernel, [((5,) + shape, BF)], [act] + act_recv + [ast[1]], S_SCRATCH,
                hbm_in=(5,), hbm_out=(0,), aliases={5: 0}, nbytes=W_BYTES,
            )
            asw[1] = flip(after(ast[1], zsw[1]), "pipe", 1)
            part = after(part, asw[1])
            (gh,) = call(last_kernel, [(half_shape, BF)], [part] + recv + [slope[0]], nbytes=1 << 18)
            pairs[0] = (g, gh)
            break
        gh, part, *outs = call(
            functools.partial(mid_kernel, layer), [(half_shape, BF)] + part_outs,
            [part] + recv + [slope[layer], all_up], W_SCRATCH,
            hbm_in=(6,), flops=flops // 2, nbytes=W_BYTES,
        )
        pairs[layer] = (g, gh)
        recv = partners(outs)
        if layer > 1:
            act_recv.append(flip(after(act, part), "tensor", 1 << len(act_recv)))
            part = after(part, act_recv[-1])
        else:
            zsw[0] = flip(after(zst[0], part), "pipe", 1)
            asw[0] = flip(after(ast[0], zsw[0]), "pipe", 1)
            part = after(part, asw[0])
        g, part, *outs = call(
            functools.partial(end_kernel, layer - 1), [(half_shape, BF)] + part_outs,
            [part] + recv + [g, all_down], W_SCRATCH,
            hbm_in=(6,), flops=flops // 2, nbytes=W_BYTES,
        )
    packed = [jnp.concatenate(pr, axis=1) for pr in pairs]
    low, high = jnp.stack(packed[:2]), jnp.stack(packed[2:])
    mine = jnp.where(h == 0, low, high)
    got = flip(jnp.where(h == 0, high, low), "pipe", 2)
    full = jnp.where(h == 0, jnp.concatenate([mine, got], 1), jnp.concatenate([got, mine], 1))
    g_own = jnp.where(c == 0, full[0], full[1])
    g_oth = flip(jnp.where(c == 0, full[1], full[0]), "pipe", 1)
    (partial,) = call(
        grad_kernel,
        [((4, 2, 3 * BS, BS), BF)],
        [g_own, g_oth] + zst + zsw + ast + asw,
        [pltpu.VMEM((4, 5) + shape, BF), pltpu.SemaphoreType.DMA((4,))],
        hbm_in=tuple(range(2, 10)),
        flops=8 * flops,
        nbytes=6 << 20,
        limit=24 << 20,
    )
    acc = lax.dynamic_index_in_dim(partial, d, 0, keepdims=False).astype(F32)
    for k in (1, 2, 3):
        acc = acc + flip(lax.dynamic_index_in_dim(partial, d ^ k, 0, keepdims=False), "dp", k).astype(F32)
    acc = acc.astype(BF)
    quarters = [acc] + [flip(acc, "dp", k) for k in (1, 2, 3)]
    up, down = call(place_kernel, [((12 * BS, BS), F32)] * 2, quarters, nbytes=10 << 20, limit=24 << 20)
    out = (1, 2, 6, BS, BS)
    return up.reshape(out), down.reshape(out)


def solution(mesh):
    acts = P(None, "dp", "tensor")
    weights = P("pipe", "tensor", None, None, None)
    return jax.shard_map(
        per_device, mesh=mesh, in_specs=(acts, acts, weights, weights), out_specs=(weights, weights), check_vma=False
    )
```

```python
import functools

import jax
import jax.numpy as jnp
from jax import lax
from jax.experimental import pallas as pl
from jax.experimental.pallas import tpu as pltpu
from jax.sharding import PartitionSpec as P

ROOT_HALF = 0.7071067811865476
INV_ROOT_TWO_PI = 0.3989422804014327
BS = 256
BF = jnp.bfloat16
F32 = jnp.float32
ANY = pl.BlockSpec(memory_space=pl.ANY)
VMEM = pl.BlockSpec(memory_space=pltpu.VMEM)
HBM = pl.BlockSpec(memory_space=pltpu.HBM)
NN = (((1,), (0,)), ((), ()))
NT = (((1,), (1,)), ((), ()))
TN = (((0,), (0,)), ((), ()))


def dot(a, b, dims):
    return lax.dot_general(a, b, dims, preferred_element_type=F32)


def flip(x, axis, bit):
    n = lax.axis_size(axis)
    return lax.ppermute(x, axis, [(i, i ^ bit) for i in range(n)])


def after(x, *events):
    return lax.optimization_barrier((x,) + events)[0]


def partners(arrays):
    return [flip(a, "tensor", 1 << b) for b, a in enumerate(arrays)]


def fetch(which, sources, wbuf, sems):
    for s, src in enumerate(sources):

        @pl.when(which == s)
        def _():
            for j in range(2):
                pltpu.make_async_copy(src.at[j], wbuf.at[j], sems.at[j]).start()


def arrived(j, sources, wbuf, sems):
    pltpu.make_async_copy(sources[0].at[j], wbuf.at[j], sems.at[j]).wait()
    return wbuf[j].reshape(6 * BS, BS)


def own_and_partner(j, own, recv):
    cols = pl.ds(j * BS, BS)
    flipped = pl.ds((1 - j) * BS, BS)
    return jnp.concatenate([own[:, cols], own[:, flipped]] + [r[:, cols] for r in recv], axis=1)


def stack_copies(own, recv, stack, sem):
    return [pltpu.make_async_copy(src, stack.at[i], sem.at[i]) for i, src in enumerate([own] + recv)]


def layer_source(q, keep):
    p = lax.axis_index("pipe")
    return (p % 2) ^ q, p // 2 if keep else 1


def up_kernel(n_src, keep, q, *refs):
    which, write = layer_source(q, keep)
    own, recv, refs = refs[0], list(refs[1:5]), refs[5:]
    sources, refs = refs[:n_src], refs[n_src:]
    if keep:
        (_, old_slope), refs = refs[:2], refs[2:]
    act, slope, stack, wbuf, sems, ssem = refs
    fetch(which, sources, wbuf, sems)
    copies = stack_copies(own, recv, stack, ssem)

    @pl.when(write == 1)
    def _():
        for cp in copies:
            cp.start()

    for j in range(2):
        x = own_and_partner(j, own, recv)
        w = arrived(j, sources, wbuf, sems)
        hid = dot(x, w, NN)
        cdf = 0.5 * (1.0 + lax.erf(hid * ROOT_HALF))
        cols = pl.ds(j * BS, BS)
        act[:, cols] = (hid * cdf).astype(BF)
        s = (cdf + hid * INV_ROOT_TWO_PI * jnp.exp(-0.5 * hid * hid)).astype(BF)
        if keep:
            s = jnp.where(write == 1, s, old_slope[:, cols])
        slope[:, cols] = s

    @pl.when(write == 1)
    def _():
        for cp in copies:
            cp.wait()


def down_kernel(n_src, keep, q, *refs):
    which, write = layer_source(q, keep)
    z, own, recv, refs = refs[0], refs[1], list(refs[2:6]), refs[6:]
    sources, refs = refs[:n_src], refs[n_src:]
    if keep:
        refs = refs[1:]
    znew, stack, wbuf, sems, ssem = refs
    fetch(which, sources, wbuf, sems)
    copies = stack_copies(own, recv, stack, ssem)

    @pl.when(write == 1)
    def _():
        for cp in copies:
            cp.start()

    for j in range(2):
        x = own_and_partner(j, own, recv)
        w = arrived(j, sources, wbuf, sems)
        cols = pl.ds(j * BS, BS)
        znew[:, cols] = (z[:, cols].astype(F32) + dot(x, w, NN)).astype(BF)

    @pl.when(write == 1)
    def _():
        for cp in copies:
            cp.wait()


def stack_kernel(own, r0, r1, r2, r3, _, stack, ssem):
    write = lax.axis_index("pipe") // 2
    copies = stack_copies(own, [r0, r1, r2, r3], stack, ssem)

    @pl.when(write == 1)
    def _():
        for cp in copies:
            cp.start()
        for cp in copies:
            cp.wait()


def fetch_layer(layer, wall, wbuf, sems):
    for j in range(2):
        pltpu.make_async_copy(wall.at[layer, j], wbuf.at[j], sems.at[j]).start()


def products(g, wall, wbuf, sems, part, outs):
    rows = g.shape[0]
    acc = [None, None]
    for j in range(2):
        w = arrived(j, [wall.at[0]], wbuf, sems)
        t = dot(g[:, j * BS : (j + 1) * BS], w, NT)
        acc[j] = t[:, :BS] if acc[j] is None else acc[j] + t[:, :BS]
        other = t[:, BS : 2 * BS]
        acc[1 - j] = other if acc[1 - j] is None else acc[1 - j] + other
        for k, o in enumerate(outs):
            o[:, j * BS : (j + 1) * BS] = t[:, (k + 2) * BS : (k + 3) * BS].astype(BF)
    for j in range(2):
        part[:, j * BS : (j + 1) * BS] = acc[j]


def first_kernel(layer, g, wall, part, o0, o1, o2, o3, wbuf, sems):
    fetch_layer(layer, wall, wbuf, sems)
    products(g[...], wall, wbuf, sems, part, (o0, o1, o2, o3))


def total(part, recv):
    s = part[...]
    for r in recv:
        s = s + r[...].astype(F32)
    return s


def mid_kernel(layer, part, r0, r1, r2, r3, slope, wall, gh, newpart, o0, o1, o2, o3, wbuf, sems):
    fetch_layer(layer, wall, wbuf, sems)
    v = (total(part, (r0, r1, r2, r3)) * slope[...].astype(F32)).astype(BF)
    gh[...] = v
    products(v, wall, wbuf, sems, newpart, (o0, o1, o2, o3))


def end_kernel(layer, part, r0, r1, r2, r3, g, wall, gnew, newpart, o0, o1, o2, o3, wbuf, sems):
    fetch_layer(layer, wall, wbuf, sems)
    v = (total(part, (r0, r1, r2, r3)) + g[...].astype(F32)).astype(BF)
    gnew[...] = v
    products(v, wall, wbuf, sems, newpart, (o0, o1, o2, o3))


def last_kernel(part, r0, r1, r2, r3, slope, gh):
    gh[...] = (total(part, (r0, r1, r2, r3)) * slope[...].astype(F32)).astype(BF)


def token_products(buf, src_of, g, out):
    for j in range(2):
        gj = g[:, j * BS : (j + 1) * BS]
        for k in range(6):
            src = 0 if k < 2 else k - 1
            src_of(src)
            xc = pl.ds((1 - j if k == 1 else j) * BS, BS)
            out(j, k, dot(buf[src, :, xc], gj, TN).astype(BF))


def near_grad_kernel(g_keep, g_recv, for_low, for_high, x_recv, out, buf, sems):
    rows = g_keep.shape[0]
    for which, src in enumerate((for_low, for_high)):

        @pl.when(lax.axis_index("pipe") % 2 == which)
        def _():
            pltpu.make_async_copy(src, buf.at[:, pl.ds(0, rows)], sems.at[0]).start()

    second = pltpu.make_async_copy(x_recv, buf.at[:, pl.ds(rows, rows)], sems.at[1])
    second.start()
    pltpu.make_async_copy(for_low, buf.at[:, pl.ds(0, rows)], sems.at[0]).wait()
    second.wait()

    def put(j, k, v):
        out[2 * j + k // 3, (k % 3) * BS : (k % 3 + 1) * BS, :] = v

    g = jnp.concatenate([g_keep[...], g_recv[...]], axis=0)
    token_products(buf, lambda src: None, g, put)


def far_grad_kernel(g_keep, g_recv, gathered, out, buf, g, sems):
    rows = g_keep.shape[1]
    d = lax.axis_index("dp")
    copies = [
        [
            pltpu.make_async_copy(
                gathered.at[d ^ k, src], buf.at[src, pl.ds(2 * rows * k, 2 * rows)], sems.at[src, k]
            )
            for k in range(4)
        ]
        for src in range(5)
    ]
    for group in copies:
        for cp in group:
            cp.start()
    for k in range(4):
        g[2 * rows * k : 2 * rows * k + rows, :] = g_keep[k]
        g[2 * rows * k + rows : 2 * rows * (k + 1), :] = g_recv[k]
    seen = set()

    def ready(src):
        if src not in seen:
            seen.add(src)
            for cp in copies[src]:
                cp.wait()

    def put(j, k, v):
        out[(6 * j + k) * BS : (6 * j + k + 1) * BS, :] = v

    token_products(buf, ready, g, put)


def join_kernel(far, q0, q1, q2, q3, up, send):
    quarters = [
        (pl.ds(pl.multiple_of((lax.axis_index("dp") ^ k) * 3 * BS, 3 * BS), 3 * BS), q)
        for k, q in enumerate((q0, q1, q2, q3))
    ]

    @pl.when(lax.axis_index("pipe") % 2 == 0)
    def _():
        up[...] = far[...].astype(F32)
        for rows, q in quarters:
            send[rows, :] = q[...]

    @pl.when(lax.axis_index("pipe") % 2 == 1)
    def _():
        send[...] = far[...]
        for rows, q in quarters:
            up[rows, :] = q[...].astype(F32)


def call(body, outs, ins, scratch=(), any_in=(), hbm_in=(), hbm_out=(), aliases=None, flops=0, nbytes=0, limit=12 << 20):
    return pl.pallas_call(
        body,
        out_shape=[pltpu.HBM(s, t) if i in hbm_out else jax.ShapeDtypeStruct(s, t) for i, (s, t) in enumerate(outs)],
        in_specs=[ANY if i in any_in else HBM if i in hbm_in else VMEM for i in range(len(ins))],
        out_specs=[HBM if i in hbm_out else VMEM for i in range(len(outs))],
        scratch_shapes=list(scratch),
        input_output_aliases=aliases or {},
        compiler_params=pltpu.CompilerParams(vmem_limit_bytes=limit),
        cost_estimate=pl.CostEstimate(flops=flops, bytes_accessed=nbytes, transcendentals=0),
    )(*[pltpu.with_memory_space_constraint(x, pltpu.HBM) if i in hbm_in else x for i, x in enumerate(ins)])


W_SCRATCH = [pltpu.VMEM((2, 6, BS, BS), BF), pltpu.SemaphoreType.DMA((2,))]
S_SCRATCH = [pltpu.SemaphoreType.DMA((5,))]
W_BYTES = 12 * BS * BS * 2


def per_device(inputs, cotangent, up_weight, down_weight):
    p = lax.axis_index("pipe")
    d = lax.axis_index("dp")
    h, c = p // 2, p % 2
    rows, width = inputs.shape[1], inputs.shape[2]
    half = rows // 2
    shape, half_shape = (rows, width), (half, width)
    flops = 2 * rows * 6 * BS * width

    ups, downs = [up_weight[0]], [down_weight[0]]
    all_down = lax.all_gather(downs[0], "pipe")

    def fwd_up(stage, q, z, recv):
        keep = stage == 1
        return call(
            functools.partial(up_kernel, 2, keep, q),
            [(shape, BF), (shape, BF), ((5,) + shape, BF)],
            [z] + recv + ups[:2] + ([zst[q], slopes[q]] if keep else []),
            W_SCRATCH + S_SCRATCH,
            hbm_in=(5, 6, 7),
            hbm_out=(2,),
            aliases={7: 2} if keep else None,
            flops=flops,
            nbytes=2 * W_BYTES,
        )

    def fwd_down(stage, q, z, act, recv):
        keep = stage == 1
        return call(
            functools.partial(down_kernel, 2, keep, q),
            [(shape, BF), ((5,) + shape, BF)],
            [z, act] + recv + downs[:2] + ([ast[q]] if keep else []),
            W_SCRATCH + S_SCRATCH,
            hbm_in=(6, 7, 8),
            hbm_out=(1,),
            aliases={8: 1} if keep else None,
            flops=flops,
            nbytes=2 * W_BYTES,
        )

    slopes, zst, ast = [None, None], [None, None], [None, None]
    z = lax.dynamic_index_in_dim(inputs, c, 0, keepdims=False)
    recv = partners([z] * 4)
    ups.append(flip(after(ups[0], z), "pipe", 1))
    act, slopes[0], zst[0] = fwd_up(0, 0, z, recv)
    recv = partners([act] * 4)
    downs.append(flip(after(downs[0], act), "pipe", 1))
    z, ast[0] = fwd_down(0, 0, z, act, recv)
    recv = partners([z] * 4)
    act, slopes[1], zst[1] = fwd_up(0, 1, z, recv)
    recv = partners([act] * 4)
    z, ast[1] = fwd_down(0, 1, z, act, recv)
    g = lax.dynamic_slice_in_dim(lax.dynamic_index_in_dim(cotangent, c, 0, keepdims=False), h * half, half, 0)
    part_outs = [(half_shape, F32)] + [(half_shape, BF)] * 4
    part, *outs = call(
        functools.partial(first_kernel, 3), part_outs, [after(g, act), all_down], W_SCRATCH,
        hbm_in=(1,), flops=flops // 2, nbytes=W_BYTES,
    )
    z = after(flip(z, "pipe", 2), part)
    first_recv = partners(outs)
    z = after(z, *first_recv)
    all_up = lax.all_gather(after(ups[0], z), "pipe")
    recv = partners([z] * 4)
    act, slopes[0], zst[0] = fwd_up(1, 0, z, recv)
    recv = partners([act] * 4)
    z, ast[0] = fwd_down(1, 0, z, act, recv)
    recv = partners([z] * 4)
    act, slopes[1], zst[1] = fwd_up(1, 1, z, recv)
    near = flip(after(jnp.where(c == 0, ast[0], zst[0]), z), "pipe", 1)
    gathered = lax.all_gather(
        jnp.concatenate([jnp.where(c == 0, zst[0], ast[0]), near], axis=1), "dp"
    )

    both = jnp.stack(slopes)
    mine = lax.dynamic_slice_in_dim(both, h * half, half, 1)
    got = flip(lax.dynamic_slice_in_dim(both, (1 - h) * half, half, 1), "pipe", 2)
    low, high = jnp.where(h == 0, mine, got), jnp.where(h == 0, got, mine)
    slope = [low[0], low[1], high[0], high[1]]

    def both_halves(low, high):
        mine = jnp.where(h == 0, low, high)
        got = flip(jnp.where(h == 0, high, low), "pipe", 2)
        return jnp.where(h == 0, jnp.concatenate([mine, got]), jnp.concatenate([got, mine]))

    gs, ghs, act_recv = {3: g}, {}, []

    def send_act(part):
        act_recv.append(flip(after(act, part), "tensor", 1 << len(act_recv)))
        return after(part, act_recv[-1])

    def backward(kernel, layer, part, recv, other, weights):
        return call(
            functools.partial(kernel, layer), [(half_shape, BF)] + part_outs,
            [part] + recv + [other, weights], W_SCRATCH,
            hbm_in=(6,), flops=flops // 2, nbytes=W_BYTES,
        )

    ghs[3], part, *outs = backward(mid_kernel, 3, part, first_recv, slope[3], all_up)
    recv, part = partners(outs), send_act(part)
    gs[2], part, *outs = backward(end_kernel, 2, part, recv, gs[3], all_down)
    recv, part = partners(outs), send_act(part)
    ghs[2], part, *outs = backward(mid_kernel, 2, part, recv, slope[2], all_up)
    recv, part = partners(outs), send_act(part)
    gs[1], part, *outs = backward(end_kernel, 1, part, recv, gs[2], all_down)
    recv, part = partners(outs), send_act(part)
    ghs[1], part, *outs = backward(mid_kernel, 1, part, recv, slope[1], all_up)
    recv = partners(outs)
    (ast[1],) = call(
        stack_kernel, [((5,) + shape, BF)], [act] + act_recv + [ast[1]], S_SCRATCH,
        hbm_in=(5,), hbm_out=(0,), aliases={5: 0}, nbytes=W_BYTES,
    )
    x_recv = flip(after(jnp.where(c == 0, zst[1], ast[1]), part), "pipe", 1)
    odd = both_halves(
        after(jnp.concatenate([gs[1], ghs[1]], axis=1), x_recv), jnp.concatenate([gs[3], ghs[3]], axis=1)
    )
    part = after(part, odd)
    gs[0], part, *outs = backward(end_kernel, 0, part, recv, gs[1], all_down)
    recv = partners(outs)
    odd_g, odd_gh = odd[:, :width], odd[:, width:]
    (partial,) = call(
        near_grad_kernel,
        [((4, 3 * BS, BS), BF)],
        [jnp.where(c == 0, odd_g, odd_gh), flip(after(jnp.where(c == 0, odd_gh, odd_g), part), "pipe", 1)]
        + [ast[1], zst[1], x_recv],
        [pltpu.VMEM((5, 2 * rows, width), BF), pltpu.SemaphoreType.DMA((2,))],
        hbm_in=(2, 3, 4),
        flops=4 * flops,
        nbytes=3 << 20,
    )
    even_g = both_halves(gs[0], gs[2])
    part = after(part, partial, even_g)
    (ghs[0],) = call(last_kernel, [(half_shape, BF)], [part] + recv + [slope[0]], nbytes=1 << 18)
    even_gh = both_halves(ghs[0], ghs[2])

    acc = lax.dynamic_index_in_dim(partial, d, 0, keepdims=False).astype(F32)
    shares = [flip(lax.dynamic_index_in_dim(partial, d ^ k, 0, keepdims=False), "dp", k) for k in (1, 2, 3)]
    for share in shares:
        acc = acc + share.astype(F32)
    acc = acc.astype(BF)
    late_g = after(even_g, shares[0], even_gh)
    all_g = jnp.stack([even_g] + [flip(late_g, "dp", k) for k in (1, 2, 3)])
    all_gh = jnp.stack([even_gh] + [flip(even_gh, "dp", k) for k in (1, 2, 3)])
    quarters = [acc] + [flip(acc, "dp", k) for k in (1, 2, 3)]
    (far,) = call(
        far_grad_kernel,
        [((12 * BS, BS), BF)],
        [jnp.where(c == 0, all_gh, all_g), flip(jnp.where(c == 0, all_g, all_gh), "pipe", 1), gathered],
        [
            pltpu.VMEM((5, 8 * rows, width), BF),
            pltpu.VMEM((8 * rows, width), BF),
            pltpu.SemaphoreType.DMA((5, 4)),
        ],
        hbm_in=(2,),
        flops=16 * flops,
        nbytes=8 << 20,
        limit=32 << 20,
    )
    up, send = call(
        join_kernel, [((12 * BS, BS), F32), ((12 * BS, BS), BF)], [far] + quarters, nbytes=6 << 20, limit=24 << 20
    )
    down = flip(send, "pipe", 1).astype(F32)
    out = (1, 2, 6, BS, BS)
    return up.reshape(out), down.reshape(out)


def solution(mesh):
    acts = P(None, "dp", "tensor")
    weights = P("pipe", "tensor", None, None, None)
    return jax.shard_map(
        per_device, mesh=mesh, in_specs=(acts, acts, weights, weights), out_specs=(weights, weights), check_vma=False
    )
```

```python
import functools

import jax
import jax.numpy as jnp
from jax import lax
from jax.experimental import pallas as pl
from jax.experimental.pallas import tpu as pltpu
from jax.sharding import PartitionSpec as P

ROOT_HALF = 0.7071067811865476
INV_ROOT_TWO_PI = 0.3989422804014327
BS = 256
BF = jnp.bfloat16
F32 = jnp.float32
ANY = pl.BlockSpec(memory_space=pl.ANY)
VMEM = pl.BlockSpec(memory_space=pltpu.VMEM)
HBM = pl.BlockSpec(memory_space=pltpu.HBM)
NN = (((1,), (0,)), ((), ()))
NT = (((1,), (1,)), ((), ()))
TN = (((0,), (0,)), ((), ()))


def dot(a, b, dims):
    return lax.dot_general(a, b, dims, preferred_element_type=F32)


def flip(x, axis, bit):
    n = lax.axis_size(axis)
    return lax.ppermute(x, axis, [(i, i ^ bit) for i in range(n)])


def after(x, *events):
    return lax.optimization_barrier((x,) + events)[0]


def partners(arrays):
    return [flip(a, "tensor", 1 << b) for b, a in enumerate(arrays)]


def fetch(which, sources, wbuf, sems):
    for s, src in enumerate(sources):

        @pl.when(which == s)
        def _():
            for j in range(2):
                pltpu.make_async_copy(src.at[j], wbuf.at[j], sems.at[j]).start()


def arrived(j, sources, wbuf, sems):
    pltpu.make_async_copy(sources[0].at[j], wbuf.at[j], sems.at[j]).wait()
    return wbuf[j].reshape(6 * BS, BS)


def own_and_partner(j, own, recv):
    cols = pl.ds(j * BS, BS)
    flipped = pl.ds((1 - j) * BS, BS)
    return jnp.concatenate([own[:, cols], own[:, flipped]] + [r[:, cols] for r in recv], axis=1)


def stack_copies(own, recv, stack, sem):
    return [pltpu.make_async_copy(src, stack.at[i], sem.at[i]) for i, src in enumerate([own] + recv)]


def layer_source(q, keep):
    p = lax.axis_index("pipe")
    return (p % 2) ^ q, p // 2 if keep else 1


def up_kernel(n_src, keep, q, *refs):
    which, write = layer_source(q, keep)
    own, recv, refs = refs[0], list(refs[1:5]), refs[5:]
    sources, refs = refs[:n_src], refs[n_src:]
    if keep:
        (_, old_slope), refs = refs[:2], refs[2:]
    act, slope, stack, wbuf, sems, ssem = refs
    fetch(which, sources, wbuf, sems)
    copies = stack_copies(own, recv, stack, ssem)

    @pl.when(write == 1)
    def _():
        for cp in copies:
            cp.start()

    for j in range(2):
        x = own_and_partner(j, own, recv)
        w = arrived(j, sources, wbuf, sems)
        hid = dot(x, w, NN)
        cdf = 0.5 * (1.0 + lax.erf(hid * ROOT_HALF))
        cols = pl.ds(j * BS, BS)
        act[:, cols] = (hid * cdf).astype(BF)
        s = (cdf + hid * INV_ROOT_TWO_PI * jnp.exp(-0.5 * hid * hid)).astype(BF)
        if keep:
            s = jnp.where(write == 1, s, old_slope[:, cols])
        slope[:, cols] = s

    @pl.when(write == 1)
    def _():
        for cp in copies:
            cp.wait()


def down_kernel(n_src, keep, q, *refs):
    which, write = layer_source(q, keep)
    z, own, recv, refs = refs[0], refs[1], list(refs[2:6]), refs[6:]
    sources, refs = refs[:n_src], refs[n_src:]
    if keep:
        refs = refs[1:]
    znew, stack, wbuf, sems, ssem = refs
    fetch(which, sources, wbuf, sems)
    copies = stack_copies(own, recv, stack, ssem)

    @pl.when(write == 1)
    def _():
        for cp in copies:
            cp.start()

    for j in range(2):
        x = own_and_partner(j, own, recv)
        w = arrived(j, sources, wbuf, sems)
        cols = pl.ds(j * BS, BS)
        znew[:, cols] = (z[:, cols].astype(F32) + dot(x, w, NN)).astype(BF)

    @pl.when(write == 1)
    def _():
        for cp in copies:
            cp.wait()


def stack_kernel(own, r0, r1, r2, r3, _, stack, ssem):
    write = lax.axis_index("pipe") // 2
    copies = stack_copies(own, [r0, r1, r2, r3], stack, ssem)

    @pl.when(write == 1)
    def _():
        for cp in copies:
            cp.start()
        for cp in copies:
            cp.wait()


def fetch_layer(layer, wall, wbuf, sems):
    for j in range(2):
        pltpu.make_async_copy(wall.at[layer, j], wbuf.at[j], sems.at[j]).start()


def products(g, wall, wbuf, sems, part, outs):
    rows = g.shape[0]
    acc = [None, None]
    for j in range(2):
        w = arrived(j, [wall.at[0]], wbuf, sems)
        t = dot(g[:, j * BS : (j + 1) * BS], w, NT)
        acc[j] = t[:, :BS] if acc[j] is None else acc[j] + t[:, :BS]
        other = t[:, BS : 2 * BS]
        acc[1 - j] = other if acc[1 - j] is None else acc[1 - j] + other
        for k, o in enumerate(outs):
            o[:, j * BS : (j + 1) * BS] = t[:, (k + 2) * BS : (k + 3) * BS].astype(BF)
    for j in range(2):
        part[:, j * BS : (j + 1) * BS] = acc[j]


def first_kernel(layer, g, wall, part, o0, o1, o2, o3, wbuf, sems):
    fetch_layer(layer, wall, wbuf, sems)
    products(g[...], wall, wbuf, sems, part, (o0, o1, o2, o3))


def total(part, recv):
    s = part[...]
    for r in recv:
        s = s + r[...].astype(F32)
    return s


def mid_kernel(layer, part, r0, r1, r2, r3, slope, wall, gh, newpart, o0, o1, o2, o3, wbuf, sems):
    fetch_layer(layer, wall, wbuf, sems)
    v = (total(part, (r0, r1, r2, r3)) * slope[...].astype(F32)).astype(BF)
    gh[...] = v
    products(v, wall, wbuf, sems, newpart, (o0, o1, o2, o3))


def end_kernel(layer, part, r0, r1, r2, r3, g, wall, gnew, newpart, o0, o1, o2, o3, wbuf, sems):
    fetch_layer(layer, wall, wbuf, sems)
    v = (total(part, (r0, r1, r2, r3)) + g[...].astype(F32)).astype(BF)
    gnew[...] = v
    products(v, wall, wbuf, sems, newpart, (o0, o1, o2, o3))


def last_kernel(part, r0, r1, r2, r3, slope, gh):
    gh[...] = (total(part, (r0, r1, r2, r3)) * slope[...].astype(F32)).astype(BF)


def token_products(buf, src_of, g, out):
    for j in range(2):
        gj = g[:, j * BS : (j + 1) * BS]
        for k in range(6):
            src = 0 if k < 2 else k - 1
            src_of(src)
            xc = pl.ds((1 - j if k == 1 else j) * BS, BS)
            row = (6 * j + k) * BS
            out[row : row + BS, :] = dot(buf[src, :, xc], gj, TN)


def grad_kernel(g_keep, g_recv, gathered, out, buf, g, sems):
    rows = g_keep.shape[1]
    d = lax.axis_index("dp")
    copies = [
        [
            pltpu.make_async_copy(
                gathered.at[d ^ k, src], buf.at[src, pl.ds(2 * rows * k, 2 * rows)], sems.at[src, k]
            )
            for k in range(4)
        ]
        for src in range(5)
    ]
    for group in copies:
        for cp in group:
            cp.start()
    for k in range(4):
        g[2 * rows * k : 2 * rows * k + rows, :] = g_keep[k]
        g[2 * rows * k + rows : 2 * rows * (k + 1), :] = g_recv[k]
    seen = set()

    def ready(src):
        if src not in seen:
            seen.add(src)
            for cp in copies[src]:
                cp.wait()

    token_products(buf, ready, g, out)


def call(body, outs, ins, scratch=(), any_in=(), hbm_in=(), hbm_out=(), aliases=None, flops=0, nbytes=0, limit=12 << 20):
    return pl.pallas_call(
        body,
        out_shape=[pltpu.HBM(s, t) if i in hbm_out else jax.ShapeDtypeStruct(s, t) for i, (s, t) in enumerate(outs)],
        in_specs=[ANY if i in any_in else HBM if i in hbm_in else VMEM for i in range(len(ins))],
        out_specs=[HBM if i in hbm_out else VMEM for i in range(len(outs))],
        scratch_shapes=list(scratch),
        input_output_aliases=aliases or {},
        compiler_params=pltpu.CompilerParams(vmem_limit_bytes=limit),
        cost_estimate=pl.CostEstimate(flops=flops, bytes_accessed=nbytes, transcendentals=0),
    )(*[pltpu.with_memory_space_constraint(x, pltpu.HBM) if i in hbm_in else x for i, x in enumerate(ins)])


W_SCRATCH = [pltpu.VMEM((2, 6, BS, BS), BF), pltpu.SemaphoreType.DMA((2,))]
S_SCRATCH = [pltpu.SemaphoreType.DMA((5,))]
W_BYTES = 12 * BS * BS * 2


def per_device(inputs, cotangent, up_weight, down_weight):
    p = lax.axis_index("pipe")
    d = lax.axis_index("dp")
    h, c = p // 2, p % 2
    rows, width = inputs.shape[1], inputs.shape[2]
    half = rows // 2
    shape, half_shape = (rows, width), (half, width)
    flops = 2 * rows * 6 * BS * width

    ups, downs = [up_weight[0]], [down_weight[0]]
    all_down = lax.all_gather(downs[0], "pipe")

    def fwd_up(stage, q, z, recv):
        keep = stage == 1
        return call(
            functools.partial(up_kernel, 2, keep, q),
            [(shape, BF), (shape, BF), ((5,) + shape, BF)],
            [z] + recv + ups[:2] + ([zst[q], slopes[q]] if keep else []),
            W_SCRATCH + S_SCRATCH,
            hbm_in=(5, 6, 7),
            hbm_out=(2,),
            aliases={7: 2} if keep else None,
            flops=flops,
            nbytes=2 * W_BYTES,
        )

    def fwd_down(stage, q, z, act, recv):
        keep = stage == 1
        return call(
            functools.partial(down_kernel, 2, keep, q),
            [(shape, BF), ((5,) + shape, BF)],
            [z, act] + recv + downs[:2] + ([ast[q]] if keep else []),
            W_SCRATCH + S_SCRATCH,
            hbm_in=(6, 7, 8),
            hbm_out=(1,),
            aliases={8: 1} if keep else None,
            flops=flops,
            nbytes=2 * W_BYTES,
        )

    slopes, zst, ast = [None, None], [None, None], [None, None]
    z = lax.dynamic_index_in_dim(inputs, c, 0, keepdims=False)
    recv = partners([z] * 4)
    ups.append(flip(after(ups[0], z), "pipe", 1))
    act, slopes[0], zst[0] = fwd_up(0, 0, z, recv)
    recv = partners([act] * 4)
    downs.append(flip(after(downs[0], act), "pipe", 1))
    z, ast[0] = fwd_down(0, 0, z, act, recv)
    recv = partners([z] * 4)
    act, slopes[1], zst[1] = fwd_up(0, 1, z, recv)
    recv = partners([act] * 4)
    z, ast[1] = fwd_down(0, 1, z, act, recv)
    g = lax.dynamic_slice_in_dim(lax.dynamic_index_in_dim(cotangent, c, 0, keepdims=False), h * half, half, 0)
    all_up = lax.all_gather(after(ups[0], act), "pipe")
    part_outs = [(half_shape, F32)] + [(half_shape, BF)] * 4
    part, *outs = call(
        functools.partial(first_kernel, 3), part_outs, [after(g, act), all_down], W_SCRATCH,
        hbm_in=(1,), flops=flops // 2, nbytes=W_BYTES,
    )
    z = after(flip(z, "pipe", 2), part)
    first_recv = partners(outs)
    z = after(z, *first_recv)
    recv = partners([z] * 4)
    act, slopes[0], zst[0] = fwd_up(1, 0, z, recv)
    recv = partners([act] * 4)
    z, ast[0] = fwd_down(1, 0, z, act, recv)
    recv = partners([z] * 4)
    act, slopes[1], zst[1] = fwd_up(1, 1, z, recv)
    act_recv = partners([act] * 4)

    def all_tokens(pair):
        other = flip(jnp.where(c == 0, pair[1], pair[0]), "pipe", 1)
        own = jnp.where(c == 0, pair[0], pair[1])
        return lax.all_gather(jnp.concatenate([own, other], axis=1), "dp")

    all_z = all_tokens(zst)

    both = jnp.stack(slopes)
    mine = lax.dynamic_slice_in_dim(both, h * half, half, 1)
    got = flip(lax.dynamic_slice_in_dim(both, (1 - h) * half, half, 1), "pipe", 2)
    low, high = jnp.where(h == 0, mine, got), jnp.where(h == 0, got, mine)
    slope = [low[0], low[1], high[0], high[1]]

    def both_halves(low, high):
        mine = jnp.where(h == 0, low, high)
        got = flip(jnp.where(h == 0, high, low), "pipe", 2)
        return jnp.where(h == 0, jnp.concatenate([mine, got]), jnp.concatenate([got, mine]))

    gs, ghs = {3: g}, {}

    def backward(kernel, layer, part, recv, other, weights):
        return call(
            functools.partial(kernel, layer), [(half_shape, BF)] + part_outs,
            [part] + recv + [other, weights], W_SCRATCH,
            hbm_in=(6,), flops=flops // 2, nbytes=W_BYTES,
        )

    ghs[3], part, *outs = backward(mid_kernel, 3, part, first_recv, slope[3], all_up)
    (ast[1],) = call(
        stack_kernel, [((5,) + shape, BF)], [act] + act_recv + [ast[1]], S_SCRATCH,
        hbm_in=(5,), hbm_out=(0,), aliases={5: 0}, nbytes=W_BYTES,
    )
    recv, part = partners(outs), after(part, ast[1])
    gs[2], part, *outs = backward(end_kernel, 2, part, recv, gs[3], all_down)
    recv = partners(outs)
    all_a = all_tokens([ast[0], after(ast[1], part)])
    ghs[2], part, *outs = backward(mid_kernel, 2, part, recv, slope[2], all_up)
    recv = partners(outs)
    gs[1], part, *outs = backward(end_kernel, 1, part, recv, gs[2], all_down)
    recv = partners(outs)
    ghs[1], part, *outs = backward(mid_kernel, 1, part, recv, slope[1], all_up)
    recv = partners(outs)
    odd = both_halves(jnp.concatenate([gs[1], ghs[1]], axis=1), jnp.concatenate([gs[3], ghs[3]], axis=1))
    part = after(part, odd)
    gs[0], part, *outs = backward(end_kernel, 0, part, recv, gs[1], all_down)
    recv = partners(outs)
    even_g = both_halves(gs[0], gs[2])
    (ghs[0],) = call(last_kernel, [(half_shape, BF)], [after(part, even_g)] + recv + [slope[0]], nbytes=1 << 18)
    even_gh = both_halves(ghs[0], ghs[2])

    def replicas(x):
        return jnp.stack([x] + [flip(x, "dp", k) for k in (1, 2, 3)])

    def gradient(even, odd, stacks):
        (grad,) = call(
            grad_kernel,
            [((12 * BS, BS), F32)],
            [jnp.where(c == 0, even, odd), flip(jnp.where(c == 0, odd, even), "pipe", 1), stacks],
            [
                pltpu.VMEM((5, 8 * rows, width), BF),
                pltpu.VMEM((8 * rows, width), BF),
                pltpu.SemaphoreType.DMA((5, 4)),
            ],
            hbm_in=(2,),
            flops=16 * flops,
            nbytes=8 << 20,
            limit=32 << 20,
        )
        return grad

    all_odd = replicas(odd)
    down = gradient(replicas(even_g), all_odd[:, :, :width], all_a)
    up = gradient(replicas(even_gh), all_odd[:, :, width:], all_z)
    out = (1, 2, 6, BS, BS)
    return up.reshape(out), down.reshape(out)


def solution(mesh):
    acts = P(None, "dp", "tensor")
    weights = P("pipe", "tensor", None, None, None)
    return jax.shard_map(
        per_device, mesh=mesh, in_specs=(acts, acts, weights, weights), out_specs=(weights, weights), check_vma=False
    )
```

```python
import functools

import jax
import jax.numpy as jnp
from jax import lax
from jax.experimental import pallas as pl
from jax.experimental.pallas import tpu as pltpu
from jax.sharding import PartitionSpec as P

ROOT_HALF = 0.7071067811865476
INV_ROOT_TWO_PI = 0.3989422804014327
BS = 256
BF = jnp.bfloat16
F32 = jnp.float32
VMEM = pl.BlockSpec(memory_space=pltpu.VMEM)
ANY = pl.BlockSpec(memory_space=pl.ANY)
HBM = pl.BlockSpec(memory_space=pltpu.HBM)
NN = (((1,), (0,)), ((), ()))
NT = (((1,), (1,)), ((), ()))
TN = (((0,), (0,)), ((), ()))


def dot(a, b, dims):
    return lax.dot_general(a, b, dims, preferred_element_type=F32)


def flip(x, axis, bit):
    n = lax.axis_size(axis)
    return lax.ppermute(x, axis, [(i, i ^ bit) for i in range(n)])


def after(x, *events):
    return lax.optimization_barrier((x,) + events)[0]


def partners(arrays):
    return [flip(a, "tensor", 1 << b) for b, a in enumerate(arrays)]


def weights_kernel(pick, n_src, *refs):
    sources, (out, sems) = refs[:n_src], refs[n_src:]
    which = pick()

    def halves(src):
        return [pltpu.make_async_copy(src.at[j], out.at[j], sems.at[j]) for j in range(2)]

    for s, src in enumerate(sources):

        @pl.when(which == s)
        def _():
            for cp in halves(src):
                cp.start()

    for cp in halves(sources[0]):
        cp.wait()


def layer_weights_kernel(layer, wall, out, sems):
    copies = [pltpu.make_async_copy(wall.at[layer, j], out.at[j], sems.at[j]) for j in range(2)]
    for cp in copies:
        cp.start()
    for cp in copies:
        cp.wait()


def own_and_partner(j, own, recv):
    cols = pl.ds(j * BS, BS)
    flipped = pl.ds((1 - j) * BS, BS)
    return jnp.concatenate([own[:, cols], own[:, flipped]] + [r[:, cols] for r in recv], axis=1)


def stack_copies(own, recv, stack, sem):
    return [pltpu.make_async_copy(src, stack.at[i], sem.at[i]) for i, src in enumerate([own] + recv)]


def up_kernel(keep, *refs):
    write = lax.axis_index("pipe") // 2 if keep else 1
    own, recv, w, refs = refs[0], list(refs[1:5]), refs[5], refs[6:]
    if keep:
        (_, old_slope), refs = refs[:2], refs[2:]
    act, slope, stack, ssem = refs
    copies = stack_copies(own, recv, stack, ssem)

    @pl.when(write == 1)
    def _():
        for cp in copies:
            cp.start()

    for j in range(2):
        x = own_and_partner(j, own, recv)
        hid = dot(x, w[j].reshape(6 * BS, BS), NN)
        cdf = 0.5 * (1.0 + lax.erf(hid * ROOT_HALF))
        cols = pl.ds(j * BS, BS)
        act[:, cols] = (hid * cdf).astype(BF)
        s = (cdf + hid * INV_ROOT_TWO_PI * jnp.exp(-0.5 * hid * hid)).astype(BF)
        if keep:
            s = jnp.where(write == 1, s, old_slope[:, cols])
        slope[:, cols] = s

    @pl.when(write == 1)
    def _():
        for cp in copies:
            cp.wait()


def down_kernel(keep, *refs):
    write = lax.axis_index("pipe") // 2 if keep else 1
    z, own, recv, w, refs = refs[0], refs[1], list(refs[2:6]), refs[6], refs[7:]
    if keep:
        refs = refs[1:]
    znew, stack, ssem = refs
    copies = stack_copies(own, recv, stack, ssem)

    @pl.when(write == 1)
    def _():
        for cp in copies:
            cp.start()

    for j in range(2):
        x = own_and_partner(j, own, recv)
        cols = pl.ds(j * BS, BS)
        znew[:, cols] = (z[:, cols].astype(F32) + dot(x, w[j].reshape(6 * BS, BS), NN)).astype(BF)

    @pl.when(write == 1)
    def _():
        for cp in copies:
            cp.wait()


def stack_kernel(own, r0, r1, r2, r3, _, stack, ssem):
    write = lax.axis_index("pipe") // 2
    copies = stack_copies(own, [r0, r1, r2, r3], stack, ssem)

    @pl.when(write == 1)
    def _():
        for cp in copies:
            cp.start()
        for cp in copies:
            cp.wait()


def products(g, w, part, outs):
    rows = g.shape[0]
    acc = [None, None]
    for j in range(2):
        t = dot(g[:, j * BS : (j + 1) * BS], w[j].reshape(6 * BS, BS), NT)
        acc[j] = t[:, :BS] if acc[j] is None else acc[j] + t[:, :BS]
        other = t[:, BS : 2 * BS]
        acc[1 - j] = other if acc[1 - j] is None else acc[1 - j] + other
        for k, o in enumerate(outs):
            o[:, j * BS : (j + 1) * BS] = t[:, (k + 2) * BS : (k + 3) * BS].astype(BF)
    for j in range(2):
        part[:, j * BS : (j + 1) * BS] = acc[j]


def first_kernel(g, w, part, o0, o1, o2, o3):
    products(g[...], w, part, (o0, o1, o2, o3))


def total(part, recv):
    s = part[...]
    for r in recv:
        s = s + r[...].astype(F32)
    return s


def mid_kernel(part, r0, r1, r2, r3, slope, w, gh, newpart, o0, o1, o2, o3):
    v = (total(part, (r0, r1, r2, r3)) * slope[...].astype(F32)).astype(BF)
    gh[...] = v
    products(v, w, newpart, (o0, o1, o2, o3))


def end_kernel(part, r0, r1, r2, r3, g, w, gnew, newpart, o0, o1, o2, o3):
    v = (total(part, (r0, r1, r2, r3)) + g[...].astype(F32)).astype(BF)
    gnew[...] = v
    products(v, w, newpart, (o0, o1, o2, o3))


def last_kernel(part, r0, r1, r2, r3, slope, gh):
    gh[...] = (total(part, (r0, r1, r2, r3)) * slope[...].astype(F32)).astype(BF)


def token_products(buf, src_of, g, out):
    for j in range(2):
        gj = g[:, j * BS : (j + 1) * BS]
        for k in range(6):
            src = 0 if k < 2 else k - 1
            src_of(src)
            xc = pl.ds((1 - j if k == 1 else j) * BS, BS)
            row = (6 * j + k) * BS
            out[row : row + BS, :] = dot(buf[src, :, xc], gj, TN)


def grad_kernel(g_keep, g_recv, own0, own1, other0, other1, out, buf, g, sems):
    rows = g_keep.shape[1]
    first = jnp.where(lax.axis_index("pipe") % 2 == 0, lax.axis_index("dp"), 0)

    def copies(src, pair):
        return [
            pltpu.make_async_copy(
                pair[i].at[first ^ k, src], buf.at[src, pl.ds(rows * (2 * k + i), rows)], sems.at[src, 2 * k + i]
            )
            for k in range(4)
            for i in range(2)
        ]

    for which, pair in enumerate(((own0, other0), (own1, other1))):

        @pl.when(lax.axis_index("pipe") % 2 == which)
        def _():
            for src in range(5):
                for cp in copies(src, pair):
                    cp.start()

    for k in range(4):
        g[2 * rows * k : 2 * rows * k + rows, :] = g_keep[k]
        g[2 * rows * k + rows : 2 * rows * (k + 1), :] = g_recv[k]
    seen = set()

    def ready(src):
        if src not in seen:
            seen.add(src)
            for cp in copies(src, (own0, other0)):
                cp.wait()

    token_products(buf, ready, g, out)


def call(body, outs, ins, scratch=(), hbm_in=(), any_in=(), hbm_out=(), vmem_in=(), vmem_out=(), aliases=None, flops=0, nbytes=0, limit=12 << 20):
    return pl.pallas_call(
        body,
        out_shape=[pltpu.HBM(s, t) if i in hbm_out else pltpu.VMEM(s, t) if i in vmem_out else jax.ShapeDtypeStruct(s, t) for i, (s, t) in enumerate(outs)],
        in_specs=[HBM if i in hbm_in else ANY if i in any_in else VMEM for i in range(len(ins))],
        out_specs=[HBM if i in hbm_out else VMEM for i in range(len(outs))],
        scratch_shapes=list(scratch),
        input_output_aliases=aliases or {},
        compiler_params=pltpu.CompilerParams(vmem_limit_bytes=limit),
        cost_estimate=pl.CostEstimate(flops=flops, bytes_accessed=nbytes, transcendentals=0),
    )(
        *[
            pltpu.with_memory_space_constraint(x, pltpu.HBM if i in hbm_in else pltpu.VMEM)
            if i in hbm_in or i in vmem_in
            else x
            for i, x in enumerate(ins)
        ]
    )


S_SCRATCH = [pltpu.SemaphoreType.DMA((5,))]
W_BYTES = 12 * BS * BS * 2


def per_device(inputs, cotangent, up_weight, down_weight):
    p = lax.axis_index("pipe")
    d = lax.axis_index("dp")
    h, c = p // 2, p % 2
    rows, width = inputs.shape[1], inputs.shape[2]
    half = rows // 2
    shape, half_shape = (rows, width), (half, width)
    flops = 2 * rows * 6 * BS * width

    ups, downs = [up_weight[0]], [down_weight[0]]
    all_down = lax.all_gather(downs[0], "pipe")

    def load(body, sources, event):
        (w,) = call(
            body, [((2, 6, BS, BS), BF)], [after(x, event) for x in sources], [pltpu.SemaphoreType.DMA((2,))],
            hbm_in=(0,), any_in=(1,), vmem_out=(0,), nbytes=W_BYTES, limit=4 << 20,
        )
        return w

    def near_weights(q, sources, event):
        return load(functools.partial(weights_kernel, lambda: (lax.axis_index("pipe") % 2) ^ q, 2), sources, event)

    def far_weights(layer, wall, event):
        return load(functools.partial(layer_weights_kernel, layer), [wall], event)

    def fwd_up(stage, q, z, recv):
        keep = stage == 1
        w = near_weights(q, ups[:2], z)
        return call(
            functools.partial(up_kernel, keep),
            [(shape, BF), (shape, BF), ((5,) + shape, BF)],
            [z] + recv + [w] + ([zst[q], slopes[q]] if keep else []),
            S_SCRATCH,
            hbm_in=(6,) if keep else (),
            hbm_out=(2,),
            vmem_in=(5,),
            aliases={6: 2} if keep else None,
            flops=flops,
            nbytes=2 * W_BYTES,
        )

    def fwd_down(stage, q, z, act, recv):
        keep = stage == 1
        w = near_weights(q, downs[:2], act)
        return call(
            functools.partial(down_kernel, keep),
            [(shape, BF), ((5,) + shape, BF)],
            [z, act] + recv + [w] + ([ast[q]] if keep else []),
            S_SCRATCH,
            hbm_in=(7,) if keep else (),
            hbm_out=(1,),
            vmem_in=(6,),
            aliases={7: 1} if keep else None,
            flops=flops,
            nbytes=2 * W_BYTES,
        )

    slopes, zst, ast = [None, None], [None, None], [None, None]
    z = lax.dynamic_index_in_dim(inputs, c, 0, keepdims=False)
    recv = partners([z] * 4)
    ups.append(flip(after(ups[0], z), "pipe", 1))
    act, slopes[0], zst[0] = fwd_up(0, 0, z, recv)
    recv = partners([act] * 4)
    downs.append(flip(after(downs[0], act), "pipe", 1))
    z, ast[0] = fwd_down(0, 0, z, act, recv)
    recv = partners([z] * 4)
    act, slopes[1], zst[1] = fwd_up(0, 1, z, recv)
    recv = partners([act] * 4)
    z, ast[1] = fwd_down(0, 1, z, act, recv)
    g = lax.dynamic_slice_in_dim(lax.dynamic_index_in_dim(cotangent, c, 0, keepdims=False), h * half, half, 0)
    all_up = lax.all_gather(after(ups[0], act), "pipe")
    part_outs = [(half_shape, F32)] + [(half_shape, BF)] * 4
    part, *outs = call(
        first_kernel, part_outs, [after(g, act), far_weights(3, all_down, z)],
        vmem_in=(1,), flops=flops // 2, nbytes=W_BYTES,
    )
    z = after(flip(z, "pipe", 2), part)
    first_recv = partners(outs)
    z = after(z, *first_recv)
    recv = partners([z] * 4)
    act, slopes[0], zst[0] = fwd_up(1, 0, z, recv)
    recv = partners([act] * 4)
    z, ast[0] = fwd_down(1, 0, z, act, recv)
    recv = partners([z] * 4)
    act, slopes[1], zst[1] = fwd_up(1, 1, z, recv)
    act_recv = partners([act] * 4)

    zall, aall = [lax.all_gather(zst[0], "dp"), None], [lax.all_gather(ast[0], "dp"), None]
    zall[1] = lax.all_gather(zst[1], "dp")

    both = jnp.stack(slopes)
    mine = lax.dynamic_slice_in_dim(both, h * half, half, 1)
    got = flip(lax.dynamic_slice_in_dim(both, (1 - h) * half, half, 1), "pipe", 2)
    low, high = jnp.where(h == 0, mine, got), jnp.where(h == 0, got, mine)
    slope = [low[0], low[1], high[0], high[1]]

    def both_halves(low, high):
        mine = jnp.where(h == 0, low, high)
        got = flip(jnp.where(h == 0, high, low), "pipe", 2)
        return jnp.where(h == 0, jnp.concatenate([mine, got]), jnp.concatenate([got, mine]))

    gs, ghs = {3: g}, {}

    def backward(kernel, layer, part, recv, other, weights):
        return call(
            kernel, [(half_shape, BF)] + part_outs,
            [part] + recv + [other, far_weights(layer, weights, part)],
            vmem_in=(6,), flops=flops // 2, nbytes=W_BYTES,
        )

    ghs[3], part, *outs = backward(mid_kernel, 3, part, first_recv, slope[3], all_up)
    (ast[1],) = call(
        stack_kernel, [((5,) + shape, BF)], [act] + act_recv + [ast[1]], S_SCRATCH,
        hbm_in=(5,), hbm_out=(0,), aliases={5: 0}, nbytes=W_BYTES,
    )
    recv, part = partners(outs), after(part, ast[1])
    gs[2], part, *outs = backward(end_kernel, 2, part, recv, gs[3], all_down)
    recv = partners(outs)
    aall[1] = lax.all_gather(ast[1], "dp")
    zsw, asw = [flip(after(zall[0], recv[0]), "pipe", 1), None], [None, None]
    ghs[2], part, *outs = backward(mid_kernel, 2, part, recv, slope[2], all_up)
    recv = partners(outs)
    gs[1], part, *outs = backward(end_kernel, 1, after(part, zsw[0]), recv, gs[2], all_down)
    recv = partners(outs)
    asw[0] = flip(after(aall[0], recv[0]), "pipe", 1)
    ghs[1], part, *outs = backward(mid_kernel, 1, part, recv, slope[1], all_up)
    recv = partners(outs)
    gate = recv[0]
    odd = both_halves(jnp.concatenate([gs[1], ghs[1]], axis=1), jnp.concatenate([gs[3], ghs[3]], axis=1))
    zsw[1] = flip(after(zall[1], gate), "pipe", 1)
    gs[0], part, *outs = backward(end_kernel, 0, after(part, asw[0], odd), recv, gs[1], all_down)
    recv = partners(outs)
    even_g = both_halves(gs[0], gs[2])
    (ghs[0],) = call(last_kernel, [(half_shape, BF)], [after(part, zsw[1], even_g)] + recv + [slope[0]], nbytes=1 << 18)
    all_odd = lax.all_gather(after(odd, ghs[0]), "dp")
    asw[1] = flip(after(aall[1], ghs[0]), "pipe", 1)
    even_gh = both_halves(ghs[0], ghs[2])

    def gradient(even, odd, own, other):
        (grad,) = call(
            grad_kernel,
            [((12 * BS, BS), F32)],
            [jnp.where(c == 0, even, odd), flip(jnp.where(c == 0, odd, even), "pipe", 1)] + own + other,
            [
                pltpu.VMEM((5, 8 * rows, width), BF),
                pltpu.VMEM((8 * rows, width), BF),
                pltpu.SemaphoreType.DMA((5, 8)),
            ],
            hbm_in=(2, 3),
            any_in=(4, 5),
            flops=16 * flops,
            nbytes=8 << 20,
            limit=32 << 20,
        )
        return grad

    all_g, all_gh = [jnp.stack([x] + [flip(x, "dp", k) for k in (1, 2, 3)]) for x in (even_g, even_gh)]
    down = gradient(all_g, all_odd[:, :, :width], aall, asw)
    up = gradient(all_gh, all_odd[:, :, width:], zall, zsw)
    out = (1, 2, 6, BS, BS)
    return up.reshape(out), down.reshape(out)


def solution(mesh):
    acts = P(None, "dp", "tensor")
    weights = P("pipe", "tensor", None, None, None)
    return jax.shard_map(
        per_device, mesh=mesh, in_specs=(acts, acts, weights, weights), out_specs=(weights, weights), check_vma=False
    )
```

```python
import functools

import jax
import jax.numpy as jnp
from jax import lax
from jax.experimental import pallas as pl
from jax.experimental.pallas import tpu as pltpu
from jax.sharding import PartitionSpec as P

ROOT_HALF = 0.7071067811865476
INV_ROOT_TWO_PI = 0.3989422804014327
BS = 256
BF = jnp.bfloat16
F32 = jnp.float32
VMEM = pl.BlockSpec(memory_space=pltpu.VMEM)
ANY = pl.BlockSpec(memory_space=pl.ANY)
HBM = pl.BlockSpec(memory_space=pltpu.HBM)
NN = (((1,), (0,)), ((), ()))
NT = (((1,), (1,)), ((), ()))
TN = (((0,), (0,)), ((), ()))


def dot(a, b, dims):
    return lax.dot_general(a, b, dims, preferred_element_type=F32)


def flip(x, axis, bit):
    n = lax.axis_size(axis)
    return lax.ppermute(x, axis, [(i, i ^ bit) for i in range(n)])


def after(x, *events):
    return lax.optimization_barrier((x,) + events)[0]


def partners(arrays):
    return [flip(a, "tensor", 1 << b) for b, a in enumerate(arrays)]


def weights_kernel(pick, n_src, *refs):
    sources, (out, sems) = refs[:n_src], refs[n_src:]
    which = pick()

    def halves(src):
        return [pltpu.make_async_copy(src.at[j], out.at[j], sems.at[j]) for j in range(2)]

    for s, src in enumerate(sources):

        @pl.when(which == s)
        def _():
            for cp in halves(src):
                cp.start()

    for cp in halves(sources[0]):
        cp.wait()


def layer_weights_kernel(layer, wall, out, sems):
    copies = [pltpu.make_async_copy(wall.at[layer, j], out.at[j], sems.at[j]) for j in range(2)]
    for cp in copies:
        cp.start()
    for cp in copies:
        cp.wait()


def own_and_partner(j, own, recv):
    cols = pl.ds(j * BS, BS)
    flipped = pl.ds((1 - j) * BS, BS)
    return jnp.concatenate([own[:, cols], own[:, flipped]] + [r[:, cols] for r in recv], axis=1)


def stack_copies(own, recv, stack, sem):
    return [pltpu.make_async_copy(src, stack.at[i], sem.at[i]) for i, src in enumerate([own] + recv)]


def up_kernel(keep, *refs):
    write = lax.axis_index("pipe") // 2 if keep else 1
    own, recv, w, refs = refs[0], list(refs[1:5]), refs[5], refs[6:]
    if keep:
        (_, old_slope), refs = refs[:2], refs[2:]
    act, slope, stack, ssem = refs
    copies = stack_copies(own, recv, stack.at[0], ssem)

    @pl.when(write == 1)
    def _():
        for cp in copies:
            cp.start()

    for j in range(2):
        x = own_and_partner(j, own, recv)
        hid = dot(x, w[j].reshape(6 * BS, BS), NN)
        cdf = 0.5 * (1.0 + lax.erf(hid * ROOT_HALF))
        cols = pl.ds(j * BS, BS)
        act[:, cols] = (hid * cdf).astype(BF)
        s = (cdf + hid * INV_ROOT_TWO_PI * jnp.exp(-0.5 * hid * hid)).astype(BF)
        if keep:
            s = jnp.where(write == 1, s, old_slope[:, cols])
        slope[:, cols] = s

    @pl.when(write == 1)
    def _():
        for cp in copies:
            cp.wait()


def down_kernel(keep, *refs):
    write = lax.axis_index("pipe") // 2 if keep else 1
    z, own, recv, w, refs = refs[0], refs[1], list(refs[2:6]), refs[6], refs[7:]
    _, znew, stack, ssem = refs
    copies = stack_copies(own, recv, stack.at[1], ssem)

    @pl.when(write == 1)
    def _():
        for cp in copies:
            cp.start()

    for j in range(2):
        x = own_and_partner(j, own, recv)
        cols = pl.ds(j * BS, BS)
        znew[:, cols] = (z[:, cols].astype(F32) + dot(x, w[j].reshape(6 * BS, BS), NN)).astype(BF)

    @pl.when(write == 1)
    def _():
        for cp in copies:
            cp.wait()


def stack_kernel(own, r0, r1, r2, r3, _, stack, ssem):
    write = lax.axis_index("pipe") // 2
    copies = stack_copies(own, [r0, r1, r2, r3], stack.at[1], ssem)

    @pl.when(write == 1)
    def _():
        for cp in copies:
            cp.start()
        for cp in copies:
            cp.wait()


def products(g, w, part, outs):
    rows = g.shape[0]
    acc = [None, None]
    for j in range(2):
        t = dot(g[:, j * BS : (j + 1) * BS], w[j].reshape(6 * BS, BS), NT)
        acc[j] = t[:, :BS] if acc[j] is None else acc[j] + t[:, :BS]
        other = t[:, BS : 2 * BS]
        acc[1 - j] = other if acc[1 - j] is None else acc[1 - j] + other
        for k, o in enumerate(outs):
            o[:, j * BS : (j + 1) * BS] = t[:, (k + 2) * BS : (k + 3) * BS].astype(BF)
    for j in range(2):
        part[:, j * BS : (j + 1) * BS] = acc[j]


def first_kernel(g, w, part, o0, o1, o2, o3):
    products(g[...], w, part, (o0, o1, o2, o3))


def total(part, recv):
    s = part[...]
    for r in recv:
        s = s + r[...].astype(F32)
    return s


def mid_kernel(part, r0, r1, r2, r3, slope, w, gh, newpart, o0, o1, o2, o3):
    v = (total(part, (r0, r1, r2, r3)) * slope[...].astype(F32)).astype(BF)
    gh[...] = v
    products(v, w, newpart, (o0, o1, o2, o3))


def end_kernel(part, r0, r1, r2, r3, g, w, gnew, newpart, o0, o1, o2, o3):
    v = (total(part, (r0, r1, r2, r3)) + g[...].astype(F32)).astype(BF)
    gnew[...] = v
    products(v, w, newpart, (o0, o1, o2, o3))


def last_kernel(part, r0, r1, r2, r3, slope, gh):
    gh[...] = (total(part, (r0, r1, r2, r3)) * slope[...].astype(F32)).astype(BF)


def gather_kernel(kind, own0, own1, other0, other1, out, sems):
    rows = out.shape[1] // 8
    first = lax.axis_index("dp")

    def copies(pair):
        return [
            pltpu.make_async_copy(
                pair[i].at[first ^ k, kind], out.at[:, pl.ds(rows * (2 * k + i), rows)], sems.at[2 * k + i]
            )
            for k in range(4)
            for i in range(2)
        ]

    for which, pair in enumerate(((own0, other0), (own1, other1))):

        @pl.when(lax.axis_index("pipe") % 2 == which)
        def _():
            for cp in copies(pair):
                cp.start()

    for cp in copies((own0, other0)):
        cp.wait()


def grad_kernel(g_keep, g_recv, stack, out, g):
    rows = g_keep.shape[1]
    for k in range(4):
        g[2 * rows * k : 2 * rows * k + rows, :] = g_keep[k]
        g[2 * rows * k + rows : 2 * rows * (k + 1), :] = g_recv[k]
    for j in range(2):
        gj = g[:, j * BS : (j + 1) * BS]
        for k in range(6):
            xc = pl.ds((1 - j if k == 1 else j) * BS, BS)
            row = (6 * j + k) * BS
            out[row : row + BS, :] = dot(stack[0 if k < 2 else k - 1, :, xc], gj, TN)


def call(body, outs, ins, scratch=(), hbm_in=(), any_in=(), hbm_out=(), vmem_in=(), vmem_out=(), aliases=None, flops=0, nbytes=0, limit=12 << 20):
    return pl.pallas_call(
        body,
        out_shape=[pltpu.HBM(s, t) if i in hbm_out else pltpu.VMEM(s, t) if i in vmem_out else jax.ShapeDtypeStruct(s, t) for i, (s, t) in enumerate(outs)],
        in_specs=[HBM if i in hbm_in else ANY if i in any_in else VMEM for i in range(len(ins))],
        out_specs=[HBM if i in hbm_out else VMEM for i in range(len(outs))],
        scratch_shapes=list(scratch),
        input_output_aliases=aliases or {},
        compiler_params=pltpu.CompilerParams(vmem_limit_bytes=limit),
        cost_estimate=pl.CostEstimate(flops=flops, bytes_accessed=nbytes, transcendentals=0),
    )(
        *[
            pltpu.with_memory_space_constraint(x, pltpu.HBM if i in hbm_in else pltpu.VMEM)
            if i in hbm_in or i in vmem_in
            else x
            for i, x in enumerate(ins)
        ]
    )


S_SCRATCH = [pltpu.SemaphoreType.DMA((5,))]
W_BYTES = 12 * BS * BS * 2


def per_device(inputs, cotangent, up_weight, down_weight):
    p = lax.axis_index("pipe")
    d = lax.axis_index("dp")
    h, c = p // 2, p % 2
    rows, width = inputs.shape[1], inputs.shape[2]
    half = rows // 2
    shape, half_shape = (rows, width), (half, width)
    flops = 2 * rows * 6 * BS * width

    ups, downs = [up_weight[0]], [down_weight[0]]
    all_down = lax.all_gather(downs[0], "pipe")

    def load(body, sources, event):
        (w,) = call(
            body, [((2, 6, BS, BS), BF)], [after(x, event) for x in sources], [pltpu.SemaphoreType.DMA((2,))],
            hbm_in=(0,), any_in=(1,), vmem_out=(0,), nbytes=W_BYTES, limit=4 << 20,
        )
        return w

    def near_weights(q, sources, event):
        return load(functools.partial(weights_kernel, lambda: (lax.axis_index("pipe") % 2) ^ q, 2), sources, event)

    def far_weights(layer, wall, event):
        return load(functools.partial(layer_weights_kernel, layer), [wall], event)

    def fwd_up(stage, q, z, recv):
        keep = stage == 1
        w = near_weights(q, ups[:2], z)
        return call(
            functools.partial(up_kernel, keep),
            [(shape, BF), (shape, BF), ((2, 5) + shape, BF)],
            [z] + recv + [w] + ([stacks[q], slopes[q]] if keep else []),
            S_SCRATCH,
            hbm_in=(6,) if keep else (),
            hbm_out=(2,),
            vmem_in=(5,),
            aliases={6: 2} if keep else None,
            flops=flops,
            nbytes=2 * W_BYTES,
        )

    def fwd_down(stage, q, z, act, recv):
        keep = stage == 1
        w = near_weights(q, downs[:2], act)
        return call(
            functools.partial(down_kernel, keep),
            [(shape, BF), ((2, 5) + shape, BF)],
            [z, act] + recv + [w, stacks[q]],
            S_SCRATCH,
            hbm_in=(7,),
            hbm_out=(1,),
            vmem_in=(6,),
            aliases={7: 1},
            flops=flops,
            nbytes=2 * W_BYTES,
        )

    slopes, stacks = [None, None], [None, None]
    z = lax.dynamic_index_in_dim(inputs, c, 0, keepdims=False)
    recv = partners([z] * 4)
    ups.append(flip(after(ups[0], z), "pipe", 1))
    act, slopes[0], stacks[0] = fwd_up(0, 0, z, recv)
    recv = partners([act] * 4)
    downs.append(flip(after(downs[0], act), "pipe", 1))
    z, stacks[0] = fwd_down(0, 0, z, act, recv)
    recv = partners([z] * 4)
    act, slopes[1], stacks[1] = fwd_up(0, 1, z, recv)
    recv = partners([act] * 4)
    z, stacks[1] = fwd_down(0, 1, z, act, recv)
    g = lax.dynamic_slice_in_dim(lax.dynamic_index_in_dim(cotangent, c, 0, keepdims=False), h * half, half, 0)
    all_up = lax.all_gather(after(ups[0], act), "pipe")
    part_outs = [(half_shape, F32)] + [(half_shape, BF)] * 4
    part, *outs = call(
        first_kernel, part_outs, [after(g, act), far_weights(3, all_down, z)],
        vmem_in=(1,), flops=flops // 2, nbytes=W_BYTES,
    )
    z = after(flip(z, "pipe", 2), part)
    first_recv = partners(outs)
    z = after(z, *first_recv)
    recv = partners([z] * 4)
    act, slopes[0], stacks[0] = fwd_up(1, 0, z, recv)
    recv = partners([act] * 4)
    z, stacks[0] = fwd_down(1, 0, z, act, recv)
    recv = partners([z] * 4)
    act, slopes[1], stacks[1] = fwd_up(1, 1, z, recv)
    act_recv = partners([act] * 4)

    gathered = [lax.all_gather(stacks[0], "dp")]

    both = jnp.stack(slopes)
    mine = lax.dynamic_slice_in_dim(both, h * half, half, 1)
    got = flip(lax.dynamic_slice_in_dim(both, (1 - h) * half, half, 1), "pipe", 2)
    low, high = jnp.where(h == 0, mine, got), jnp.where(h == 0, got, mine)
    slope = [low[0], low[1], high[0], high[1]]

    def both_halves(low, high):
        mine = jnp.where(h == 0, low, high)
        got = flip(jnp.where(h == 0, high, low), "pipe", 2)
        return jnp.where(h == 0, jnp.concatenate([mine, got]), jnp.concatenate([got, mine]))

    def replicas(x):
        return jnp.stack([x] + [flip(x, "dp", k) for k in (1, 2, 3)])

    gs, ghs = {3: g}, {}

    def backward(kernel, layer, part, recv, other, weights):
        return call(
            kernel, [(half_shape, BF)] + part_outs,
            [part] + recv + [other, far_weights(layer, weights, part)],
            vmem_in=(6,), flops=flops // 2, nbytes=W_BYTES,
        )

    ghs[3], part, *outs = backward(mid_kernel, 3, part, first_recv, slope[3], all_up)
    (stacks[1],) = call(
        stack_kernel, [((2, 5) + shape, BF)], [act] + act_recv + [stacks[1]], S_SCRATCH,
        hbm_in=(5,), hbm_out=(0,), aliases={5: 0}, nbytes=W_BYTES,
    )
    recv, part = partners(outs), after(part, stacks[1])
    gs[2], part, *outs = backward(end_kernel, 2, part, recv, gs[3], all_down)
    recv = partners(outs)
    gathered.append(lax.all_gather(after(stacks[1], part), "dp"))
    ghs[2], part, *outs = backward(mid_kernel, 2, part, recv, slope[2], all_up)
    recv = partners(outs)
    gs[1], part, *outs = backward(end_kernel, 1, part, recv, gs[2], all_down)
    recv = partners(outs)
    ghs[1], part, *outs = backward(mid_kernel, 1, part, recv, slope[1], all_up)
    recv = partners(outs)
    swapped = [flip(after(gathered[0], part), "pipe", 1)]
    odd = both_halves(jnp.concatenate([gs[1], ghs[1]], axis=1), jnp.concatenate([gs[3], ghs[3]], axis=1))
    gs[0], part, *outs = backward(end_kernel, 0, after(part, odd), recv, gs[1], all_down)
    recv = partners(outs)
    all_odd = replicas(odd)
    even_g = both_halves(gs[0], gs[2])
    (ghs[0],) = call(last_kernel, [(half_shape, BF)], [after(part, even_g, swapped[0])] + recv + [slope[0]], nbytes=1 << 18)
    swapped.append(flip(after(gathered[1], ghs[0]), "pipe", 1))
    even_gh = both_halves(ghs[0], ghs[2])

    def gradient(even, odd, kind):
        (stack,) = call(
            functools.partial(gather_kernel, kind), [((5, 8 * rows, width), BF)], gathered + swapped,
            [pltpu.SemaphoreType.DMA((8,))], hbm_in=(0, 1), any_in=(2, 3), vmem_out=(0,), nbytes=10 << 20, limit=4 << 20,
        )
        (grad,) = call(
            grad_kernel,
            [((12 * BS, BS), F32)],
            [jnp.where(c == 0, even, odd), flip(jnp.where(c == 0, odd, even), "pipe", 1), stack],
            [pltpu.VMEM((8 * rows, width), BF)],
            vmem_in=(2,),
            flops=16 * flops,
            nbytes=8 << 20,
            limit=16 << 20,
        )
        return grad

    down = gradient(replicas(after(even_g, even_gh)), all_odd[:, :, :width], 1)
    up = gradient(replicas(even_gh), all_odd[:, :, width:], 0)
    out = (1, 2, 6, BS, BS)
    return up.reshape(out), down.reshape(out)


def solution(mesh):
    acts = P(None, "dp", "tensor")
    weights = P("pipe", "tensor", None, None, None)
    return jax.shard_map(
        per_device, mesh=mesh, in_specs=(acts, acts, weights, weights), out_specs=(weights, weights), check_vma=False
    )
```

```python
import functools

import jax
import jax.numpy as jnp
from jax import lax
from jax.experimental import pallas as pl
from jax.experimental.pallas import tpu as pltpu
from jax.sharding import PartitionSpec as P

ROOT_HALF = 0.7071067811865476
INV_ROOT_TWO_PI = 0.3989422804014327
BS = 256
BF = jnp.bfloat16
F32 = jnp.float32
VMEM = pl.BlockSpec(memory_space=pltpu.VMEM)
ANY = pl.BlockSpec(memory_space=pl.ANY)
HBM = pl.BlockSpec(memory_space=pltpu.HBM)
NN = (((1,), (0,)), ((), ()))
NT = (((1,), (1,)), ((), ()))
TN = (((0,), (0,)), ((), ()))


def dot(a, b, dims):
    return lax.dot_general(a, b, dims, preferred_element_type=F32)


def flip(x, axis, bit):
    n = lax.axis_size(axis)
    return lax.ppermute(x, axis, [(i, i ^ bit) for i in range(n)])


def after(x, *events):
    return lax.optimization_barrier((x,) + events)[0]


def partners(arrays):
    return [flip(a, "tensor", 1 << b) for b, a in enumerate(arrays)]


def weights_kernel(pick, n_src, *refs):
    sources, (out, sems) = refs[:n_src], refs[n_src:]
    which = pick()

    def halves(src):
        return [pltpu.make_async_copy(src.at[j], out.at[j], sems.at[j]) for j in range(2)]

    for s, src in enumerate(sources):

        @pl.when(which == s)
        def _():
            for cp in halves(src):
                cp.start()

    for cp in halves(sources[0]):
        cp.wait()


def layer_weights_kernel(layer, wall, out, sems):
    copies = [pltpu.make_async_copy(wall.at[layer, j], out.at[j], sems.at[j]) for j in range(2)]
    for cp in copies:
        cp.start()
    for cp in copies:
        cp.wait()


def own_and_partner(j, own, recv):
    cols = pl.ds(j * BS, BS)
    flipped = pl.ds((1 - j) * BS, BS)
    return jnp.concatenate([own[:, cols], own[:, flipped]] + [r[:, cols] for r in recv], axis=1)


def stack_copies(own, recv, stack, sem):
    return [pltpu.make_async_copy(src, stack.at[i], sem.at[i]) for i, src in enumerate([own] + recv)]


def up_kernel(keep, *refs):
    write = lax.axis_index("pipe") // 2 if keep else 1
    own, recv, w, refs = refs[0], list(refs[1:5]), refs[5], refs[6:]
    if keep:
        (_, old_slope), refs = refs[:2], refs[2:]
    act, slope, stack, ssem = refs
    copies = stack_copies(own, recv, stack.at[0], ssem)

    @pl.when(write == 1)
    def _():
        for cp in copies:
            cp.start()

    for j in range(2):
        x = own_and_partner(j, own, recv)
        hid = dot(x, w[j].reshape(6 * BS, BS), NN)
        cdf = 0.5 * (1.0 + lax.erf(hid * ROOT_HALF))
        cols = pl.ds(j * BS, BS)
        act[:, cols] = (hid * cdf).astype(BF)
        s = (cdf + hid * INV_ROOT_TWO_PI * jnp.exp(-0.5 * hid * hid)).astype(BF)
        if keep:
            s = jnp.where(write == 1, s, old_slope[:, cols])
        slope[:, cols] = s

    @pl.when(write == 1)
    def _():
        for cp in copies:
            cp.wait()


def down_kernel(keep, *refs):
    write = lax.axis_index("pipe") // 2 if keep else 1
    z, own, recv, w, refs = refs[0], refs[1], list(refs[2:6]), refs[6], refs[7:]
    _, znew, stack, ssem = refs
    copies = stack_copies(own, recv, stack.at[1], ssem)

    @pl.when(write == 1)
    def _():
        for cp in copies:
            cp.start()

    for j in range(2):
        x = own_and_partner(j, own, recv)
        cols = pl.ds(j * BS, BS)
        znew[:, cols] = (z[:, cols].astype(F32) + dot(x, w[j].reshape(6 * BS, BS), NN)).astype(BF)

    @pl.when(write == 1)
    def _():
        for cp in copies:
            cp.wait()


def stack_kernel(own, r0, r1, r2, r3, _, stack, ssem):
    write = lax.axis_index("pipe") // 2
    copies = stack_copies(own, [r0, r1, r2, r3], stack.at[1], ssem)

    @pl.when(write == 1)
    def _():
        for cp in copies:
            cp.start()
        for cp in copies:
            cp.wait()


def products(g, w, part, outs):
    rows = g.shape[0]
    acc = [None, None]
    for j in range(2):
        t = dot(g[:, j * BS : (j + 1) * BS], w[j].reshape(6 * BS, BS), NT)
        acc[j] = t[:, :BS] if acc[j] is None else acc[j] + t[:, :BS]
        other = t[:, BS : 2 * BS]
        acc[1 - j] = other if acc[1 - j] is None else acc[1 - j] + other
        for k, o in enumerate(outs):
            o[:, j * BS : (j + 1) * BS] = t[:, (k + 2) * BS : (k + 3) * BS].astype(BF)
    for j in range(2):
        part[:, j * BS : (j + 1) * BS] = acc[j]


def first_kernel(g, w, part, o0, o1, o2, o3):
    products(g[...], w, part, (o0, o1, o2, o3))


def total(part, recv):
    s = part[...]
    for r in recv:
        s = s + r[...].astype(F32)
    return s


def mid_kernel(part, r0, r1, r2, r3, slope, w, gh, newpart, o0, o1, o2, o3):
    v = (total(part, (r0, r1, r2, r3)) * slope[...].astype(F32)).astype(BF)
    gh[...] = v
    products(v, w, newpart, (o0, o1, o2, o3))


def end_kernel(part, r0, r1, r2, r3, g, w, gnew, newpart, o0, o1, o2, o3):
    v = (total(part, (r0, r1, r2, r3)) + g[...].astype(F32)).astype(BF)
    gnew[...] = v
    products(v, w, newpart, (o0, o1, o2, o3))


def last_kernel(part, r0, r1, r2, r3, slope, gh):
    gh[...] = (total(part, (r0, r1, r2, r3)) * slope[...].astype(F32)).astype(BF)


def gather_kernel(kind, own0, own1, other0, other1, out, sems):
    rows = out.shape[1] // 8
    first = lax.axis_index("dp")

    def copies(pair):
        return [
            pltpu.make_async_copy(
                pair[i].at[first ^ k, kind], out.at[:, pl.ds(rows * (2 * k + i), rows)], sems.at[2 * k + i]
            )
            for k in range(4)
            for i in range(2)
        ]

    for which, pair in enumerate(((own0, other0), (own1, other1))):

        @pl.when(lax.axis_index("pipe") % 2 == which)
        def _():
            for cp in copies(pair):
                cp.start()

    for cp in copies((own0, other0)):
        cp.wait()


def grad_kernel(g_keep, g_recv, stack, out, g):
    rows = g_keep.shape[1]
    for k in range(4):
        g[2 * rows * k : 2 * rows * k + rows, :] = g_keep[k]
        g[2 * rows * k + rows : 2 * rows * (k + 1), :] = g_recv[k]
    for j in range(2):
        gj = g[:, j * BS : (j + 1) * BS]
        for k in range(6):
            xc = pl.ds((1 - j if k == 1 else j) * BS, BS)
            row = (6 * j + k) * BS
            out[row : row + BS, :] = dot(stack[0 if k < 2 else k - 1, :, xc], gj, TN)


def call(body, outs, ins, scratch=(), hbm_in=(), any_in=(), hbm_out=(), vmem_in=(), vmem_out=(), aliases=None, flops=0, nbytes=0, limit=12 << 20):
    return pl.pallas_call(
        body,
        out_shape=[pltpu.HBM(s, t) if i in hbm_out else pltpu.VMEM(s, t) if i in vmem_out else jax.ShapeDtypeStruct(s, t) for i, (s, t) in enumerate(outs)],
        in_specs=[HBM if i in hbm_in else ANY if i in any_in else VMEM for i in range(len(ins))],
        out_specs=[HBM if i in hbm_out else VMEM for i in range(len(outs))],
        scratch_shapes=list(scratch),
        input_output_aliases=aliases or {},
        compiler_params=pltpu.CompilerParams(vmem_limit_bytes=limit),
        cost_estimate=pl.CostEstimate(flops=flops, bytes_accessed=nbytes, transcendentals=0),
    )(
        *[
            pltpu.with_memory_space_constraint(x, pltpu.HBM if i in hbm_in else pltpu.VMEM)
            if i in hbm_in or i in vmem_in
            else x
            for i, x in enumerate(ins)
        ]
    )


S_SCRATCH = [pltpu.SemaphoreType.DMA((5,))]
W_BYTES = 12 * BS * BS * 2


def per_device(inputs, cotangent, up_weight, down_weight):
    p = lax.axis_index("pipe")
    d = lax.axis_index("dp")
    h, c = p // 2, p % 2
    rows, width = inputs.shape[1], inputs.shape[2]
    half = rows // 2
    shape, half_shape = (rows, width), (half, width)
    flops = 2 * rows * 6 * BS * width

    ups, downs = [up_weight[0]], [down_weight[0]]
    all_down = lax.all_gather(downs[0], "pipe")

    def load(body, sources, event):
        (w,) = call(
            body, [((2, 6, BS, BS), BF)], [after(x, event) for x in sources], [pltpu.SemaphoreType.DMA((2,))],
            hbm_in=(0,), any_in=(1,), vmem_out=(0,), nbytes=W_BYTES, limit=4 << 20,
        )
        return w

    def near_weights(q, sources, event):
        return load(functools.partial(weights_kernel, lambda: (lax.axis_index("pipe") % 2) ^ q, 2), sources, event)

    def far_weights(layer, wall, event):
        return load(functools.partial(layer_weights_kernel, layer), [wall], event)

    def fwd_up(stage, q, z, recv):
        keep = stage == 1
        w = near_weights(q, ups[:2], z)
        return call(
            functools.partial(up_kernel, keep),
            [(shape, BF), (shape, BF), ((2, 5) + shape, BF)],
            [z] + recv + [w] + ([stacks[q], slopes[q]] if keep else []),
            S_SCRATCH,
            hbm_in=(6,) if keep else (),
            hbm_out=(2,),
            vmem_in=(5,),
            aliases={6: 2} if keep else None,
            flops=flops,
            nbytes=2 * W_BYTES,
        )

    def fwd_down(stage, q, z, act, recv):
        keep = stage == 1
        w = near_weights(q, downs[:2], act)
        return call(
            functools.partial(down_kernel, keep),
            [(shape, BF), ((2, 5) + shape, BF)],
            [z, act] + recv + [w, stacks[q]],
            S_SCRATCH,
            hbm_in=(7,),
            hbm_out=(1,),
            vmem_in=(6,),
            aliases={7: 1},
            flops=flops,
            nbytes=2 * W_BYTES,
        )

    slopes, stacks = [None, None], [None, None]
    z = lax.dynamic_index_in_dim(inputs, c, 0, keepdims=False)
    recv = partners([z] * 4)
    ups.append(flip(after(ups[0], z), "pipe", 1))
    act, slopes[0], stacks[0] = fwd_up(0, 0, z, recv)
    recv = partners([act] * 4)
    downs.append(flip(after(downs[0], act), "pipe", 1))
    z, stacks[0] = fwd_down(0, 0, z, act, recv)
    recv = partners([z] * 4)
    act, slopes[1], stacks[1] = fwd_up(0, 1, z, recv)
    recv = partners([act] * 4)
    z, stacks[1] = fwd_down(0, 1, z, act, recv)
    g = lax.dynamic_slice_in_dim(lax.dynamic_index_in_dim(cotangent, c, 0, keepdims=False), h * half, half, 0)
    all_up = lax.all_gather(after(ups[0], act), "pipe")
    part_outs = [(half_shape, F32)] + [(half_shape, BF)] * 4
    part, *outs = call(
        first_kernel, part_outs, [after(g, act), far_weights(3, all_down, z)],
        vmem_in=(1,), flops=flops // 2, nbytes=W_BYTES,
    )
    z = after(flip(z, "pipe", 2), part)
    first_recv = partners(outs)
    z = after(z, *first_recv)
    recv = partners([z] * 4)
    act, slopes[0], stacks[0] = fwd_up(1, 0, z, recv)
    recv = partners([act] * 4)
    z, stacks[0] = fwd_down(1, 0, z, act, recv)
    recv = partners([z] * 4)
    act, slopes[1], stacks[1] = fwd_up(1, 1, z, recv)
    act_recv = [flip(act, "tensor", 1)]

    gathered = [lax.all_gather(stacks[0], "dp")]

    both = jnp.stack(slopes)
    mine = lax.dynamic_slice_in_dim(both, h * half, half, 1)
    got = flip(lax.dynamic_slice_in_dim(both, (1 - h) * half, half, 1), "pipe", 2)
    low, high = jnp.where(h == 0, mine, got), jnp.where(h == 0, got, mine)
    slope = [low[0], low[1], high[0], high[1]]

    def both_halves(low, high):
        mine = jnp.where(h == 0, low, high)
        got = flip(jnp.where(h == 0, high, low), "pipe", 2)
        return jnp.where(h == 0, jnp.concatenate([mine, got]), jnp.concatenate([got, mine]))

    def replicas(x):
        return jnp.stack([x] + [flip(x, "dp", k) for k in (1, 2, 3)])

    gs, ghs = {3: g}, {}

    def backward(kernel, layer, part, recv, other, weights):
        return call(
            kernel, [(half_shape, BF)] + part_outs,
            [part] + recv + [other, far_weights(layer, weights, part)],
            vmem_in=(6,), flops=flops // 2, nbytes=W_BYTES,
        )

    def send_act(part):
        act_recv.append(flip(after(act, part), "tensor", 1 << len(act_recv)))
        return after(part, act_recv[-1])

    ghs[3], part, *outs = backward(mid_kernel, 3, after(part, act_recv[0]), first_recv, slope[3], all_up)
    recv, part = partners(outs), send_act(part)
    gs[2], part, *outs = backward(end_kernel, 2, part, recv, gs[3], all_down)
    recv, part = partners(outs), send_act(part)
    ghs[2], part, *outs = backward(mid_kernel, 2, part, recv, slope[2], all_up)
    recv, part = partners(outs), send_act(part)
    gs[1], part, *outs = backward(end_kernel, 1, part, recv, gs[2], all_down)
    recv = partners(outs)
    (stacks[1],) = call(
        stack_kernel, [((2, 5) + shape, BF)], [after(act, part)] + act_recv + [stacks[1]], S_SCRATCH,
        hbm_in=(5,), hbm_out=(0,), aliases={5: 0}, nbytes=W_BYTES,
    )
    gathered.append(lax.all_gather(stacks[1], "dp"))
    ghs[1], part, *outs = backward(mid_kernel, 1, part, recv, slope[1], all_up)
    recv = partners(outs)
    swapped = [flip(after(gathered[0], part), "pipe", 1)]
    odd = both_halves(jnp.concatenate([gs[1], ghs[1]], axis=1), jnp.concatenate([gs[3], ghs[3]], axis=1))
    gs[0], part, *outs = backward(end_kernel, 0, after(part, odd), recv, gs[1], all_down)
    recv = partners(outs)
    all_odd = replicas(odd)
    even_g = both_halves(gs[0], gs[2])
    (ghs[0],) = call(last_kernel, [(half_shape, BF)], [after(part, even_g, swapped[0])] + recv + [slope[0]], nbytes=1 << 18)
    even_gh = both_halves(ghs[0], ghs[2])
    all_gh = replicas(even_gh)
    swapped.append(flip(after(gathered[1], all_gh), "pipe", 1))

    def gradient(even, odd, kind):
        (stack,) = call(
            functools.partial(gather_kernel, kind), [((5, 8 * rows, width), BF)], gathered + swapped,
            [pltpu.SemaphoreType.DMA((8,))], hbm_in=(0, 1), any_in=(2, 3), vmem_out=(0,), nbytes=10 << 20, limit=4 << 20,
        )
        (grad,) = call(
            grad_kernel,
            [((12 * BS, BS), F32)],
            [jnp.where(c == 0, even, odd), flip(jnp.where(c == 0, odd, even), "pipe", 1), stack],
            [pltpu.VMEM((8 * rows, width), BF)],
            vmem_in=(2,),
            flops=16 * flops,
            nbytes=8 << 20,
            limit=16 << 20,
        )
        return grad

    down = gradient(replicas(after(even_g, even_gh)), all_odd[:, :, :width], 1)
    up = gradient(all_gh, all_odd[:, :, width:], 0)
    out = (1, 2, 6, BS, BS)
    return up.reshape(out), down.reshape(out)


def solution(mesh):
    acts = P(None, "dp", "tensor")
    weights = P("pipe", "tensor", None, None, None)
    return jax.shard_map(
        per_device, mesh=mesh, in_specs=(acts, acts, weights, weights), out_specs=(weights, weights), check_vma=False
    )
```

```python
import functools

import jax
import jax.numpy as jnp
from jax import lax
from jax.experimental import pallas as pl
from jax.experimental.pallas import tpu as pltpu
from jax.sharding import PartitionSpec as P

ROOT_HALF = 0.7071067811865476
INV_ROOT_TWO_PI = 0.3989422804014327
BS = 256
BF = jnp.bfloat16
F32 = jnp.float32
VMEM = pl.BlockSpec(memory_space=pltpu.VMEM)
ANY = pl.BlockSpec(memory_space=pl.ANY)
HBM = pl.BlockSpec(memory_space=pltpu.HBM)
NN = (((1,), (0,)), ((), ()))
NT = (((1,), (1,)), ((), ()))
TN = (((0,), (0,)), ((), ()))


def dot(a, b, dims):
    return lax.dot_general(a, b, dims, preferred_element_type=F32)


def flip(x, axis, bit):
    n = lax.axis_size(axis)
    return lax.ppermute(x, axis, [(i, i ^ bit) for i in range(n)])


def after(x, *events):
    return lax.optimization_barrier((x,) + events)[0]


def partners(arrays):
    return [flip(a, "tensor", 1 << b) for b, a in enumerate(arrays)]


def weights_kernel(pick, n_src, *refs):
    sources, (out, sems) = refs[:n_src], refs[n_src:]
    which = pick()

    def halves(src):
        return [pltpu.make_async_copy(src.at[j], out.at[j], sems.at[j]) for j in range(2)]

    for s, src in enumerate(sources):

        @pl.when(which == s)
        def _():
            for cp in halves(src):
                cp.start()

    for cp in halves(sources[0]):
        cp.wait()


def layer_weights_kernel(layer, wall, out, sems):
    copies = [pltpu.make_async_copy(wall.at[layer, j], out.at[j], sems.at[j]) for j in range(2)]
    for cp in copies:
        cp.start()
    for cp in copies:
        cp.wait()


def own_and_partner(j, own, recv):
    cols = pl.ds(j * BS, BS)
    flipped = pl.ds((1 - j) * BS, BS)
    return jnp.concatenate([own[:, cols], own[:, flipped]] + [r[:, cols] for r in recv], axis=1)


def stack_copies(own, recv, stack, sem):
    return [pltpu.make_async_copy(src, stack.at[i], sem.at[i]) for i, src in enumerate([own] + recv)]


def up_kernel(keep, *refs):
    write = lax.axis_index("pipe") // 2 if keep else 1
    own, recv, w, refs = refs[0], list(refs[1:5]), refs[5], refs[6:]
    if keep:
        (_, old_slope), refs = refs[:2], refs[2:]
    act, slope, stack, ssem = refs
    copies = stack_copies(own, recv, stack.at[0], ssem)

    @pl.when(write == 1)
    def _():
        for cp in copies:
            cp.start()

    for j in range(2):
        x = own_and_partner(j, own, recv)
        hid = dot(x, w[j].reshape(6 * BS, BS), NN)
        cdf = 0.5 * (1.0 + lax.erf(hid * ROOT_HALF))
        cols = pl.ds(j * BS, BS)
        act[:, cols] = (hid * cdf).astype(BF)
        s = (cdf + hid * INV_ROOT_TWO_PI * jnp.exp(-0.5 * hid * hid)).astype(BF)
        if keep:
            s = jnp.where(write == 1, s, old_slope[:, cols])
        slope[:, cols] = s

    @pl.when(write == 1)
    def _():
        for cp in copies:
            cp.wait()


def down_kernel(keep, *refs):
    write = lax.axis_index("pipe") // 2 if keep else 1
    z, own, recv, w, refs = refs[0], refs[1], list(refs[2:6]), refs[6], refs[7:]
    _, znew, stack, ssem = refs
    copies = stack_copies(own, recv, stack.at[1], ssem)

    @pl.when(write == 1)
    def _():
        for cp in copies:
            cp.start()

    for j in range(2):
        x = own_and_partner(j, own, recv)
        cols = pl.ds(j * BS, BS)
        znew[:, cols] = (z[:, cols].astype(F32) + dot(x, w[j].reshape(6 * BS, BS), NN)).astype(BF)

    @pl.when(write == 1)
    def _():
        for cp in copies:
            cp.wait()


def stack_kernel(own, r0, r1, r2, r3, _, stack, ssem):
    write = lax.axis_index("pipe") // 2
    copies = stack_copies(own, [r0, r1, r2, r3], stack.at[1], ssem)

    @pl.when(write == 1)
    def _():
        for cp in copies:
            cp.start()
        for cp in copies:
            cp.wait()


def products(g, w, part, outs):
    rows = g.shape[0]
    acc = [None, None]
    for j in range(2):
        t = dot(g[:, j * BS : (j + 1) * BS], w[j].reshape(6 * BS, BS), NT)
        acc[j] = t[:, :BS] if acc[j] is None else acc[j] + t[:, :BS]
        other = t[:, BS : 2 * BS]
        acc[1 - j] = other if acc[1 - j] is None else acc[1 - j] + other
        for k, o in enumerate(outs):
            o[:, j * BS : (j + 1) * BS] = t[:, (k + 2) * BS : (k + 3) * BS].astype(BF)
    for j in range(2):
        part[:, j * BS : (j + 1) * BS] = acc[j]


def first_kernel(g, w, part, o0, o1, o2, o3):
    products(g[...], w, part, (o0, o1, o2, o3))


def total(part, recv):
    s = part[...]
    for r in recv:
        s = s + r[...].astype(F32)
    return s


def mid_kernel(part, r0, r1, r2, r3, slope, w, gh, newpart, o0, o1, o2, o3):
    v = (total(part, (r0, r1, r2, r3)) * slope[...].astype(F32)).astype(BF)
    gh[...] = v
    products(v, w, newpart, (o0, o1, o2, o3))


def end_kernel(part, r0, r1, r2, r3, g, w, gnew, newpart, o0, o1, o2, o3):
    v = (total(part, (r0, r1, r2, r3)) + g[...].astype(F32)).astype(BF)
    gnew[...] = v
    products(v, w, newpart, (o0, o1, o2, o3))


def last_kernel(part, r0, r1, r2, r3, slope, gh):
    gh[...] = (total(part, (r0, r1, r2, r3)) * slope[...].astype(F32)).astype(BF)


def gather_kernel(kind, own0, own1, other0, other1, out, sems):
    rows = out.shape[1] // 8
    first = lax.axis_index("dp")

    def copies(pair):
        return [
            pltpu.make_async_copy(
                pair[i].at[first ^ k, kind], out.at[:, pl.ds(rows * (2 * k + i), rows)], sems.at[2 * k + i]
            )
            for k in range(4)
            for i in range(2)
        ]

    for which, pair in enumerate(((own0, other0), (own1, other1))):

        @pl.when(lax.axis_index("pipe") % 2 == which)
        def _():
            for cp in copies(pair):
                cp.start()

    for cp in copies((own0, other0)):
        cp.wait()


def grad_kernel(g_keep, g_recv, stack, out, g):
    rows = g_keep.shape[1]
    for k in range(4):
        g[2 * rows * k : 2 * rows * k + rows, :] = g_keep[k]
        g[2 * rows * k + rows : 2 * rows * (k + 1), :] = g_recv[k]
    for j in range(2):
        gj = g[:, j * BS : (j + 1) * BS]
        for k in range(6):
            xc = pl.ds((1 - j if k == 1 else j) * BS, BS)
            row = (6 * j + k) * BS
            out[row : row + BS, :] = dot(stack[0 if k < 2 else k - 1, :, xc], gj, TN)


def call(body, outs, ins, scratch=(), hbm_in=(), any_in=(), hbm_out=(), vmem_in=(), vmem_out=(), aliases=None, flops=0, nbytes=0, limit=12 << 20):
    return pl.pallas_call(
        body,
        out_shape=[pltpu.HBM(s, t) if i in hbm_out else pltpu.VMEM(s, t) if i in vmem_out else jax.ShapeDtypeStruct(s, t) for i, (s, t) in enumerate(outs)],
        in_specs=[HBM if i in hbm_in else ANY if i in any_in else VMEM for i in range(len(ins))],
        out_specs=[HBM if i in hbm_out else VMEM for i in range(len(outs))],
        scratch_shapes=list(scratch),
        input_output_aliases=aliases or {},
        compiler_params=pltpu.CompilerParams(vmem_limit_bytes=limit),
        cost_estimate=pl.CostEstimate(flops=flops, bytes_accessed=nbytes, transcendentals=0),
    )(
        *[
            pltpu.with_memory_space_constraint(x, pltpu.HBM if i in hbm_in else pltpu.VMEM)
            if i in hbm_in or i in vmem_in
            else x
            for i, x in enumerate(ins)
        ]
    )


S_SCRATCH = [pltpu.SemaphoreType.DMA((5,))]
W_BYTES = 12 * BS * BS * 2


def per_device(inputs, cotangent, up_weight, down_weight):
    p = lax.axis_index("pipe")
    d = lax.axis_index("dp")
    h, c = p // 2, p % 2
    rows, width = inputs.shape[1], inputs.shape[2]
    half = rows // 2
    shape, half_shape = (rows, width), (half, width)
    flops = 2 * rows * 6 * BS * width

    ups, downs = [up_weight[0]], [down_weight[0]]
    all_down = lax.all_gather(downs[0], "pipe")

    def load(body, sources, event):
        (w,) = call(
            body, [((2, 6, BS, BS), BF)], [after(x, event) for x in sources], [pltpu.SemaphoreType.DMA((2,))],
            hbm_in=(0,), any_in=(1,), vmem_out=(0,), nbytes=W_BYTES, limit=4 << 20,
        )
        return w

    def near_weights(q, sources, event):
        return load(functools.partial(weights_kernel, lambda: (lax.axis_index("pipe") % 2) ^ q, 2), sources, event)

    def far_weights(layer, wall, event):
        return load(functools.partial(layer_weights_kernel, layer), [wall], event)

    def fwd_up(stage, q, z, recv):
        keep = stage == 1
        w = near_weights(q, ups[:2], z)
        return call(
            functools.partial(up_kernel, keep),
            [(shape, BF), (shape, BF), ((2, 5) + shape, BF)],
            [z] + recv + [w] + ([stacks[q], slopes[q]] if keep else []),
            S_SCRATCH,
            hbm_in=(6,) if keep else (),
            hbm_out=(2,),
            vmem_in=(5,),
            aliases={6: 2} if keep else None,
            flops=flops,
            nbytes=2 * W_BYTES,
        )

    def fwd_down(stage, q, z, act, recv):
        keep = stage == 1
        w = near_weights(q, downs[:2], act)
        return call(
            functools.partial(down_kernel, keep),
            [(shape, BF), ((2, 5) + shape, BF)],
            [z, act] + recv + [w, stacks[q]],
            S_SCRATCH,
            hbm_in=(7,),
            hbm_out=(1,),
            vmem_in=(6,),
            aliases={7: 1},
            flops=flops,
            nbytes=2 * W_BYTES,
        )

    slopes, stacks = [None, None], [None, None]
    z = lax.dynamic_index_in_dim(inputs, c, 0, keepdims=False)
    recv = partners([z] * 4)
    ups.append(flip(after(ups[0], z), "pipe", 1))
    act, slopes[0], stacks[0] = fwd_up(0, 0, z, recv)
    recv = partners([act] * 4)
    downs.append(flip(after(downs[0], act), "pipe", 1))
    z, stacks[0] = fwd_down(0, 0, z, act, recv)
    recv = partners([z] * 4)
    act, slopes[1], stacks[1] = fwd_up(0, 1, z, recv)
    recv = partners([act] * 4)
    z, stacks[1] = fwd_down(0, 1, z, act, recv)
    g = lax.dynamic_slice_in_dim(lax.dynamic_index_in_dim(cotangent, c, 0, keepdims=False), h * half, half, 0)
    all_up = lax.all_gather(after(ups[0], act), "pipe")
    part_outs = [(half_shape, F32)] + [(half_shape, BF)] * 4
    part, *outs = call(
        first_kernel, part_outs, [after(g, act), far_weights(3, all_down, z)],
        vmem_in=(1,), flops=flops // 2, nbytes=W_BYTES,
    )
    z = after(flip(z, "pipe", 2), part)
    first_recv = partners(outs)
    z = after(z, *first_recv)
    recv = partners([z] * 4)
    act, slopes[0], stacks[0] = fwd_up(1, 0, z, recv)
    recv = partners([act] * 4)
    z, stacks[0] = fwd_down(1, 0, z, act, recv)
    recv = partners([z] * 4)
    act, slopes[1], stacks[1] = fwd_up(1, 1, z, recv)
    act_recv = partners([act] * 4)

    gathered = [lax.all_gather(stacks[0], "dp")]

    both = jnp.stack(slopes)
    mine = lax.dynamic_slice_in_dim(both, h * half, half, 1)
    got = flip(lax.dynamic_slice_in_dim(both, (1 - h) * half, half, 1), "pipe", 2)
    low, high = jnp.where(h == 0, mine, got), jnp.where(h == 0, got, mine)
    slope = [low[0], low[1], high[0], high[1]]

    def both_halves(low, high):
        mine = jnp.where(h == 0, low, high)
        got = flip(jnp.where(h == 0, high, low), "pipe", 2)
        return jnp.where(h == 0, jnp.concatenate([mine, got]), jnp.concatenate([got, mine]))

    def replicas(x):
        return jnp.stack([x] + [flip(x, "dp", k) for k in (1, 2, 3)])

    gs, ghs = {3: g}, {}

    def backward(kernel, layer, part, recv, other, weights):
        return call(
            kernel, [(half_shape, BF)] + part_outs,
            [part] + recv + [other, far_weights(layer, weights, part)],
            vmem_in=(6,), flops=flops // 2, nbytes=W_BYTES,
        )

    ghs[3], part, *outs = backward(mid_kernel, 3, part, first_recv, slope[3], all_up)
    (stacks[1],) = call(
        stack_kernel, [((2, 5) + shape, BF)], [act] + act_recv + [stacks[1]], S_SCRATCH,
        hbm_in=(5,), hbm_out=(0,), aliases={5: 0}, nbytes=W_BYTES,
    )
    recv, part = partners(outs), after(part, stacks[1])
    gs[2], part, *outs = backward(end_kernel, 2, part, recv, gs[3], all_down)
    recv = partners(outs)
    gathered.append(lax.all_gather(after(stacks[1], part), "dp"))
    ghs[2], part, *outs = backward(mid_kernel, 2, part, recv, slope[2], all_up)
    recv = partners(outs)
    gs[1], part, *outs = backward(end_kernel, 1, part, recv, gs[2], all_down)
    recv = partners(outs)
    ghs[1], part, *outs = backward(mid_kernel, 1, part, recv, slope[1], all_up)
    recv = partners(outs)
    swapped = [flip(after(gathered[0], part), "pipe", 1)]
    odd = both_halves(jnp.concatenate([gs[1], ghs[1]], axis=1), jnp.concatenate([gs[3], ghs[3]], axis=1))
    gs[0], part, *outs = backward(end_kernel, 0, after(part, odd), recv, gs[1], all_down)
    recv = partners(outs)
    all_odd = replicas(odd)
    even_g = both_halves(gs[0], gs[2])
    (ghs[0],) = call(last_kernel, [(half_shape, BF)], [after(part, even_g, swapped[0])] + recv + [slope[0]], nbytes=1 << 18)
    even_gh = both_halves(ghs[0], ghs[2])
    swapped.append(flip(after(gathered[1], even_gh), "pipe", 1))

    def gathered_stack(kind):
        (stack,) = call(
            functools.partial(gather_kernel, kind), [((5, 8 * rows, width), BF)], gathered + swapped,
            [pltpu.SemaphoreType.DMA((8,))], hbm_in=(0, 1), any_in=(2, 3), vmem_out=(0,), nbytes=10 << 20, limit=4 << 20,
        )
        return stack

    def gradient(even, odd, stack):
        (grad,) = call(
            grad_kernel,
            [((12 * BS, BS), F32)],
            [jnp.where(c == 0, even, odd), flip(jnp.where(c == 0, odd, even), "pipe", 1), stack],
            [pltpu.VMEM((8 * rows, width), BF)],
            vmem_in=(2,),
            flops=16 * flops,
            nbytes=8 << 20,
            limit=16 << 20,
        )
        return grad

    z_stack, act_stack = gathered_stack(0), gathered_stack(1)
    down = gradient(replicas(after(even_g, z_stack, act_stack)), all_odd[:, :, :width], act_stack)
    up = gradient(replicas(even_gh), all_odd[:, :, width:], z_stack)
    out = (1, 2, 6, BS, BS)
    return up.reshape(out), down.reshape(out)


def solution(mesh):
    acts = P(None, "dp", "tensor")
    weights = P("pipe", "tensor", None, None, None)
    return jax.shard_map(
        per_device, mesh=mesh, in_specs=(acts, acts, weights, weights), out_specs=(weights, weights), check_vma=False
    )
```
